32 devices in a mesh: grp: 2 (over x), kb: 8 (over z, y), slab: 2 (over core).
Axes of the slice: x: 2, y: 2, z: 4, core: 2. Of those that a mesh axis runs over, the one named last changes fastest.
Arguments:
- orbitals: float32 [2, 16, 32, 1024], P(None, ('grp', 'kb'), 'slab'), parts along dimension 1, may hold values from -6 to 6
- kernel: float32 [8, 32, 1024], P(None, None, 'slab'), may hold values from 0.05 to 2
- q_index: int32 [8, 8], replicated, may hold values from 0 to 7, as said below
- owner: int32 [8], replicated, may hold values from 0 to 7, each once
Outputs:
- applied: float32 [2, 16, 32, 1024], P(None, ('grp', 'kb'), 'slab'), parts along dimension 1
- gram: float32 [2, 16, 1], P(None, ('grp', 'kb')), parts along dimension 1
The draws below stay inside these ranges and needn't reach their ends.
There are 2 independent parts, one for each index of `grp`. The reference program is written for one: setup_inputs(seed, part) draws one part's arguments, and reference() takes and returns one part's arrays. A program takes and returns all parts, laid end to end along the dimension named above; an argument that names none is the same for every part. Nothing has to cross between parts.
Inputs may be any that keep to these rules, and one draw needn't show every extreme that they name: q_index[a, b] numbers the difference of k-points a and b among the 8 q vectors of the mesh: the table is symmetric, constant on its diagonal, and each row names every q once. `owner`: each block number appears once.
All inputs are finite; a program needn't handle non-finite values.
Results may differ from the reference program's by a relative error of at most 0.0003.
Values sent between devices are 32-bit elements; how exact they have to be, the bound alone decides.
No kernel may reach another device: no remote copies, remote signals or barrier semaphores. Data moves between devices by JAX's collectives and lax.ppermute only.
A program may use at most 128 MiB of HBM per device.

```python
import math
import jax
import jax.numpy as jnp
from jax import lax

G = 32
NK = 8
BAND_DEV = 1
NQ = 8
BANDS = 8
N_KB = 8


def draw_q_index(key, part):
    labels = jax.random.permutation(jax.random.fold_in(key, 11), jnp.arange(NK, dtype=jnp.int32))
    naming = jax.random.permutation(jax.random.fold_in(key, 12), jnp.arange(NK, dtype=jnp.int32))
    difference = jnp.bitwise_xor(labels[:, None], labels[None, :])
    return jnp.take(naming, difference)


def block_levels(stream_key, dims, pieces, low, top_value):
    def one(axis_at, parts):
        heights = jax.random.uniform(jax.random.fold_in(jax.random.fold_in(stream_key, 6), axis_at), (parts,), jnp.float32, low / len(pieces), top_value / len(pieces))
        return jnp.repeat(jnp.exp(heights), dims[axis_at] // parts).reshape((-1,) + (1,) * (len(dims) - axis_at - 1))

    gain = one(*pieces[0])
    for cut in pieces[1:]:
        gain = gain * one(*cut)
    return gain


def gaussian(rng, dims, spread, most, pieces=(), kind=jnp.bfloat16):
    gain = block_levels(rng, dims, pieces, -0.22, 0.18) if pieces else 1.0
    entries = jax.random.normal(rng, dims, jnp.float32) * spread * gain
    return jnp.minimum(jnp.maximum(entries, -most), most).astype(kind)


def setup_inputs(seed: int = 0, part: int = 0) -> dict:
    arg_keys = jax.random.split(jax.random.key(seed), 5)
    part_keys = jax.random.split(jax.random.fold_in(arg_keys[4], part), 5)
    return {
        "orbitals": gaussian(part_keys[0], (2, BANDS, G, G * G), 1.0, 6.0, ((1, 8), (2, 2)), jnp.float32),
        "kernel": jnp.clip(jnp.exp(math.log(2.0) - 3.6888794 * jax.random.uniform(arg_keys[1], (NQ, G, G * G), jnp.float32) ** block_levels(arg_keys[1], (NQ, G, G * G), ((2, 2),), -0.2, 0.2)), 0.05, 2.0),
        "q_index": draw_q_index(jax.random.fold_in(arg_keys[4], 71), part),
        "owner": jax.random.permutation(arg_keys[3], N_KB).astype(jnp.int32),
    }


def reference(orbitals, kernel, q_index, owner):
    band_total = orbitals.shape[1]
    wave_fns = lax.complex(orbitals[0], orbitals[1]).reshape(band_total, G, G, G)
    blocks_per_k = N_KB // NK
    band_block = jnp.repeat(owner, BAND_DEV)
    band_kpoint = band_block // blocks_per_k
    band_column = (band_block % blocks_per_k) * BAND_DEV + jnp.arange(band_total, dtype=jnp.int32) % BAND_DEV
    columns = BAND_DEV * blocks_per_k

    def one_target(target_index):
        target = wave_fns[target_index]
        spectra = jnp.fft.fftn(jnp.conj(wave_fns) * target[None], axes=(1, 2, 3))
        kernel_choice = q_index[band_kpoint[target_index], band_kpoint]
        kernel_rows = kernel[kernel_choice].reshape(band_total, G, G, G)
        potential = jnp.fft.ifftn(kernel_rows * spectra, axes=(1, 2, 3))
        applied_one = -jnp.sum(wave_fns * potential, axis=0) / NK
        correlation = jnp.sum(jnp.conj(wave_fns) * applied_one[None], axis=(1, 2, 3)) / (G * G * G)
        chosen = (band_kpoint == band_kpoint[target_index])[:, None] & (band_column[:, None] == jnp.arange(columns, dtype=jnp.int32)[None])
        gram_row = jnp.sum(jnp.where(chosen, correlation[:, None], 0.0), axis=0)
        return applied_one, gram_row

    applied_all, gram_all = lax.map(one_target, jnp.arange(band_total, dtype=jnp.int32))
    applied = jnp.stack([jnp.real(applied_all), jnp.imag(applied_all)]).reshape(2, band_total, G, G * G).astype(jnp.float32)
    gram = jnp.stack([jnp.real(gram_all), jnp.imag(gram_all)]).astype(jnp.float32)
    return applied, gram
```

```python
import functools
import math

import jax
import jax.numpy as jnp
import numpy as np
from jax import lax
from jax.experimental import pallas as pl
from jax.experimental.pallas import tpu as pltpu
from jax.sharding import PartitionSpec as P

NK = 8
LANES = 128
F32 = jnp.float32
BF16 = jnp.bfloat16


def bf16_parts(table):
    high = table.astype(np.float32).astype(BF16)
    low = (table - high.astype(np.float64)).astype(np.float32).astype(BF16)
    return np.stack([high, low])


def lane_table(side):
    lows = LANES // side
    index = np.arange(LANES)
    low, z = index // side, index % side
    phase = 2.0 * math.pi * (np.outer(low, low) / lows + np.outer(z, z) / side)
    real, imag = np.cos(phase), -np.sin(phase)
    return np.block([[real, imag], [-imag, real]])


def sublane_table(side, count):
    index = np.arange(side)
    phase = 2.0 * math.pi * (np.outer(index, index) % side) / side
    unit = np.eye(count)
    cosine, sine = np.kron(unit, np.cos(phase)), np.kron(unit, np.sin(phase))
    return np.block([[cosine, sine], [-sine, cosine]])


def twist_table(side, rows):
    tiles = side * side // LANES
    phase = 2.0 * math.pi * np.outer(np.arange(tiles), np.arange(LANES) // side) / side
    both = np.stack([np.cos(phase), np.sin(phase)], 1).astype(np.float32)
    return np.ascontiguousarray(np.broadcast_to(both[:, :, None], (tiles, 2, rows, LANES)))


def split(value):
    high = value.astype(BF16)
    return high, (value - high.astype(F32)).astype(BF16)


def dot_parts(left, right):
    dot = functools.partial(jnp.dot, preferred_element_type=F32)
    return dot(left[0], right[0]) + (dot(left[1], right[0]) + dot(left[0], right[1]))


def dft_list(values, sign):
    count = len(values)
    if count == 1:
        return values
    even, odd = dft_list(values[0::2], sign), dft_list(values[1::2], sign)
    first, second = [], []
    for k in range(count // 2):
        re, im = odd[k]
        eighth = 8 * k // count if 8 * k % count == 0 else None
        if eighth == 0:
            pass
        elif eighth == 2:
            re, im = (-im, re) if sign > 0 else (im, -re)
        elif eighth == 1:
            root = math.sqrt(0.5)
            re, im = (
                ((re - im) * root, (re + im) * root)
                if sign > 0
                else ((re + im) * root, (im - re) * root)
            )
        elif eighth == 3:
            root = math.sqrt(0.5)
            re, im = (
                ((-re - im) * root, (re - im) * root)
                if sign > 0
                else ((im - re) * root, (-re - im) * root)
            )
        else:
            angle = 2.0 * math.pi * k / count
            cosine, sine = math.cos(angle), sign * math.sin(angle)
            re, im = re * cosine - im * sine, re * sine + im * cosine
        first.append((even[k][0] + re, even[k][1] + im))
        second.append((even[k][0] - re, even[k][1] - im))
    return first + second


def lane_slice(tile):
    return pl.ds(tile * LANES, LANES)


def choose_kernel(side, choice_ref, core_ref, mine_ref, other_ref, out_ref):
    tiles = side * side // LANES
    lows = LANES // side
    scale = -1.0 / (NK * side**3)
    first_core = core_ref[0] == 0
    lane = lax.broadcasted_iota(jnp.int32, (side, LANES), 1) // side
    for pair in range(out_ref.shape[0]):
        q = choice_ref[pair]
        mine, other = mine_ref[q], other_ref[q]
        low_half = jnp.where(first_core, mine, other) * scale
        high_half = jnp.where(first_core, other, mine) * scale
        for b in range(tiles):
            total = None
            for a in range(lows):
                row = a * tiles + b
                source, chunk = row // lows, row % lows
                half = low_half if source < tiles // 2 else high_half
                at = source % (tiles // 2) * LANES
                piece = half[:, at : at + LANES]
                shift = (a - chunk) % lows * side
                if shift:
                    piece = pltpu.roll(piece, shift, 1)
                total = piece if total is None else jnp.where(lane == a, piece, total)
            out_ref[pair, :, lane_slice(b)] = total


def pair_kernel(
    side, count, has_sum, *refs
):
    refs = list(refs)
    take = lambda n: [refs.pop(0) for _ in range(n)]
    target = take(2)
    partners = [take(2) for _ in range(count)]
    (weight_ref,) = take(1)
    lane_f, lane_b, rows_f, rows_b, twist = take(5)
    sums = take(2) if has_sum else None
    outs = take(2)
    a_high, a_low, y_ref, f_high, f_low, g_ref = take(6)

    tiles = side * side // LANES
    half = side // 2
    rows = side * count

    def parts(ref):
        return ref[0], ref[1]

    for p in range(count):
        for h in range(2):
            row = p * side + h * half
            values = []
            for t in range(tiles):
                t_re, t_im = target[h][0, 0, :, lane_slice(t)], target[h][1, 0, :, lane_slice(t)]
                p_re = partners[p][h][0, 0, :, lane_slice(t)]
                p_im = partners[p][h][1, 0, :, lane_slice(t)]
                values.append((p_re * t_re + p_im * t_im, p_re * t_im - p_im * t_re))
            for b, (re, im) in enumerate(dft_list(values, -1)):
                if b:
                    cosine, sine = twist[b, 0], twist[b, 1]
                    re, im = re * cosine + im * sine, im * cosine - re * sine
                at = pl.ds(b * rows + row, half)
                for k, part in enumerate((re, im)):
                    high, low = split(part)
                    a_high[at, lane_slice(k)] = high
                    a_low[at, lane_slice(k)] = low
    y_ref[...] = dot_parts((a_high[...], a_low[...]), parts(lane_f))
    for n in range(tiles // 2):
        blocks = []
        for k in range(2):
            blocks.append(
                jnp.concatenate(
                    [y_ref[pl.ds((2 * n + j) * rows, rows), lane_slice(k)] for j in range(2)], 1
                )
            )
        spectrum = dot_parts(parts(rows_f), split(jnp.concatenate(blocks, 0)))
        weights = weight_ref[:, :, pl.ds(n * 2 * LANES, 2 * LANES)].reshape(rows, 2 * LANES)
        weighted = spectrum * jnp.concatenate([weights, weights], 0)
        back = dot_parts(parts(rows_b), split(weighted))
        high, low = split(back)
        for j in range(2):
            for k in range(2):
                at = (pl.ds((2 * n + j) * rows, rows), lane_slice(k))
                f_high[at] = high[k * rows : (k + 1) * rows, j * LANES : (j + 1) * LANES]
                f_low[at] = low[k * rows : (k + 1) * rows, j * LANES : (j + 1) * LANES]
    g_ref[...] = dot_parts((f_high[...], f_low[...]), parts(lane_b))
    gram_re = jnp.zeros((half, LANES), F32)
    gram_im = jnp.zeros((half, LANES), F32)
    for h in range(2):
        total = [[0.0, 0.0] for _ in range(tiles)]
        if has_sum:
            for t in range(tiles):
                total[t] = [sums[h][pl.ds((k * tiles + t) * half, half), :] for k in range(2)]
        for p in range(count):
            row = p * side + h * half
            values = []
            for b in range(tiles):
                at = pl.ds(b * rows + row, half)
                re, im = g_ref[at, lane_slice(0)], g_ref[at, lane_slice(1)]
                if b:
                    cosine, sine = twist[b, 0], twist[b, 1]
                    re, im = re * cosine - im * sine, im * cosine + re * sine
                values.append((re, im))
            for t, (re, im) in enumerate(dft_list(values, 1)):
                p_re = partners[p][h][0, 0, :, lane_slice(t)]
                p_im = partners[p][h][1, 0, :, lane_slice(t)]
                total[t][0] = total[t][0] + (p_re * re - p_im * im)
                total[t][1] = total[t][1] + (p_re * im + p_im * re)
        for t in range(tiles):
            re, im = total[t]
            t_re, t_im = target[h][0, 0, :, lane_slice(t)], target[h][1, 0, :, lane_slice(t)]
            gram_re += t_re * re + t_im * im
            gram_im += t_re * im - t_im * re
            outs[h][pl.ds(t * half, half), :] = re
            outs[h][pl.ds((tiles + t) * half, half), :] = im
    end = 2 * tiles * half
    scale = 1.0 / side**3
    sums_row = jnp.concatenate(
        [
            jnp.full((4, LANES), jnp.sum(gram_re) * scale, F32),
            jnp.full((4, LANES), jnp.sum(gram_im) * scale, F32),
        ],
        0,
    )
    for h in range(2):
        outs[h][pl.ds(end, 8), :] = sums_row


def join_kernel(flag_ref, mine_ref, near_ref, away_mine_ref, away_near_ref, applied_ref, gram_ref):
    half = applied_ref.shape[2]
    tiles = applied_ref.shape[3] // LANES
    own = flag_ref[0] == 1
    for k in range(2):
        for t in range(tiles):
            at = pl.ds((k * tiles + t) * half, half)
            applied_ref[k, 0, :, lane_slice(t)] = jnp.where(
                own, mine_ref[at, :], near_ref[at, :]
            ) + jnp.where(own, away_mine_ref[at, :], away_near_ref[at, :])
    end = 2 * tiles * half
    at = pl.ds(end, 8)
    sums = jnp.where(own, mine_ref[at, :], near_ref[at, :]) + jnp.where(
        own, away_mine_ref[at, :], away_near_ref[at, :]
    )
    gram_ref[0, 0, 0] = jnp.max(sums[0:1, :])
    gram_ref[1, 0, 0] = jnp.max(sums[4:5, :])


VMEM = pl.BlockSpec(memory_space=pltpu.VMEM)
SMEM = pl.BlockSpec(memory_space=pltpu.SMEM)


def params():
    return pltpu.CompilerParams(vmem_limit_bytes=48 * 2**20)


def choose(choice, core, mine, other, side):
    return pl.pallas_call(
        functools.partial(choose_kernel, side),
        out_shape=jax.ShapeDtypeStruct((choice.shape[0], side, side * side), F32),
        in_specs=[SMEM, SMEM, VMEM, VMEM],
        out_specs=VMEM,
        compiler_params=params(),
        name="choose",
    )(choice, core, mine, other)


def apply_pairs(target, partners, weights, side, sums=None):
    count = len(partners)
    half = side // 2
    tiles = side * side // LANES
    rows = side * count
    lane = lane_table(side)
    across = sublane_table(side, count)
    tables = [
        jnp.asarray(bf16_parts(lane)),
        jnp.asarray(bf16_parts(lane.T)),
        jnp.asarray(bf16_parts(across)),
        jnp.asarray(bf16_parts(across.T)),
        jnp.asarray(twist_table(side, half)),
    ]
    operands = list(target) + [x for pair in partners for x in pair] + [weights] + tables
    operands += list(sums) if sums is not None else []
    message = jax.ShapeDtypeStruct((2 * tiles * half + 8, LANES), F32)
    return pl.pallas_call(
        functools.partial(pair_kernel, side, count, sums is not None),
        out_shape=(message, message),
        in_specs=[VMEM] * len(operands),
        out_specs=(VMEM, VMEM),
        scratch_shapes=[
            pltpu.VMEM((tiles * rows, 2 * LANES), BF16),
            pltpu.VMEM((tiles * rows, 2 * LANES), BF16),
            pltpu.VMEM((tiles * rows, 2 * LANES), F32),
            pltpu.VMEM((tiles * rows, 2 * LANES), BF16),
            pltpu.VMEM((tiles * rows, 2 * LANES), BF16),
            pltpu.VMEM((tiles * rows, 2 * LANES), F32),
        ],
        compiler_params=params(),
        name="pairs",
    )(*operands)


def join(flag, parts, shape):
    return pl.pallas_call(
        join_kernel,
        out_shape=(jax.ShapeDtypeStruct(shape, F32), jax.ShapeDtypeStruct((2, 1, 1), F32)),
        in_specs=[SMEM, VMEM, VMEM, VMEM, VMEM],
        out_specs=(VMEM, SMEM),
        compiler_params=params(),
        name="join",
    )(flag, *parts)


def block_gram(orbitals, applied, owner, blocks_per_k, cells):
    highest = lax.Precision.HIGHEST
    partners = lax.all_gather(orbitals, "kb", axis=1, tiled=True)
    re = jnp.einsum("pxa,txa->tp", partners[0], applied[0], precision=highest)
    re += jnp.einsum("pxa,txa->tp", partners[1], applied[1], precision=highest)
    im = jnp.einsum("pxa,txa->tp", partners[0], applied[1], precision=highest)
    im -= jnp.einsum("pxa,txa->tp", partners[1], applied[0], precision=highest)
    sums = lax.psum(jnp.stack([re, im]) / cells, "slab")
    own = owner[lax.axis_index("kb")] // blocks_per_k
    wanted = own * blocks_per_k + jnp.arange(blocks_per_k, dtype=jnp.int32)
    selector = jnp.where(owner[:, None] == wanted[None], 1.0, 0.0).astype(F32)
    return jnp.einsum("ktp,pc->ktc", sums, selector, precision=highest)


def on_device(orbitals, kernel, q_index, owner):
    side = kernel.shape[1]
    n_kb = lax.axis_size("kb")
    lines = n_kb // 2
    blocks_per_k = n_kb // NK
    place, core = lax.axis_index("kb"), lax.axis_index("slab")
    column, line = place % 2, place // 2

    def swap(x):
        return lax.ppermute(x, "slab", [(0, 1), (1, 0)])

    def from_line(x, d):
        return lax.ppermute(
            x, "kb", [(2 * a + c, 2 * (a ^ d) + c) for a in range(lines) for c in range(2)]
        )

    beside = lax.ppermute(orbitals, "kb", [(a, a ^ 1) for a in range(n_kb)])
    mine = [orbitals] + [from_line(orbitals, d) for d in range(1, lines)]
    partners = [(x, swap(x)) for x in mine]
    home = core == column
    target_mine = jnp.where(home, orbitals, beside)
    target_sent = jnp.where(home, beside, orbitals)
    target = (target_mine, swap(target_sent))

    k_of = owner // blocks_per_k
    target_k = k_of[2 * line + core]
    partner_at = 2 * (line ^ jnp.arange(lines, dtype=jnp.int32)) + column
    choice = q_index[target_k][k_of[partner_at]]
    weights = choose(choice, core[None].astype(jnp.int32), kernel, swap(kernel), side)

    sums = None
    step = min(4, lines)
    for at in range(0, lines, step):
        sums = apply_pairs(target, partners[at : at + step], weights[at : at + step], side, sums)
    own_part, other_part = sums

    def index(line_at, column_at, core_at):
        return (2 * line_at + column_at) * 2 + core_at

    both = ("kb", "slab")
    away_mine = lax.ppermute(
        own_part,
        both,
        [(index(m, y, 1 - y), index(m, 1 - y, 1 - y)) for m in range(lines) for y in range(2)],
    )
    away_near = lax.ppermute(
        other_part,
        both,
        [(index(m, y, 1 - y), index(m, 1 - y, y)) for m in range(lines) for y in range(2)],
    )
    near = lax.ppermute(
        other_part,
        both,
        [(index(m, y, y), index(m, y, 1 - y)) for m in range(lines) for y in range(2)],
    )
    applied, gram = join(
        home[None].astype(jnp.int32), (own_part, near, away_mine, away_near), orbitals.shape
    )
    if blocks_per_k > 1:
        gram = block_gram(orbitals, applied, owner, blocks_per_k, side**3)
    return applied, gram


def solution(mesh):
    in_specs = (P(None, ("grp", "kb"), "slab", None), P(None, None, "slab"), P(), P())
    out_specs = (P(None, ("grp", "kb"), "slab", None), P(None, ("grp", "kb"), None))
    return jax.shard_map(
        on_device, mesh=mesh, in_specs=in_specs, out_specs=out_specs, check_vma=False
    )
```

```python
import functools
import math

import jax
import jax.numpy as jnp
import numpy as np
from jax import lax
from jax.experimental import pallas as pl
from jax.experimental.pallas import tpu as pltpu
from jax.sharding import PartitionSpec as P

NK = 8
LANES = 128
F32 = jnp.float32
BF16 = jnp.bfloat16


def bf16_parts(table):
    high = table.astype(np.float32).astype(BF16)
    low = (table - high.astype(np.float64)).astype(np.float32).astype(BF16)
    return np.stack([high, low])


def lane_table(side):
    lows = LANES // side
    index = np.arange(LANES)
    low, z = index // side, index % side
    phase = 2.0 * math.pi * (np.outer(low, low) / lows + np.outer(z, z) / side)
    real, imag = np.cos(phase), -np.sin(phase)
    return np.block([[real, imag], [-imag, real]])


def sublane_table(side, count):
    index = np.arange(side)
    phase = 2.0 * math.pi * (np.outer(index, index) % side) / side
    unit = np.eye(count)
    cosine, sine = np.kron(unit, np.cos(phase)), np.kron(unit, np.sin(phase))
    return np.block([[cosine, sine], [-sine, cosine]])


def twist_table(side, rows):
    tiles = side * side // LANES
    phase = 2.0 * math.pi * np.outer(np.arange(tiles), np.arange(LANES) // side) / side
    both = np.stack([np.cos(phase), np.sin(phase)], 1).astype(np.float32)
    return np.ascontiguousarray(np.broadcast_to(both[:, :, None], (tiles, 2, rows, LANES)))


def split(value):
    high = value.astype(BF16)
    return high, (value - high.astype(F32)).astype(BF16)


def dot_parts(left, right):
    dot = functools.partial(jnp.dot, preferred_element_type=F32)
    return dot(left[0], right[0]) + (dot(left[1], right[0]) + dot(left[0], right[1]))


def dft_list(values, sign):
    count = len(values)
    if count == 1:
        return values
    even, odd = dft_list(values[0::2], sign), dft_list(values[1::2], sign)
    first, second = [], []
    for k in range(count // 2):
        re, im = odd[k]
        eighth = 8 * k // count if 8 * k % count == 0 else None
        if eighth == 0:
            pass
        elif eighth == 2:
            re, im = (-im, re) if sign > 0 else (im, -re)
        elif eighth == 1:
            root = math.sqrt(0.5)
            re, im = (
                ((re - im) * root, (re + im) * root)
                if sign > 0
                else ((re + im) * root, (im - re) * root)
            )
        elif eighth == 3:
            root = math.sqrt(0.5)
            re, im = (
                ((-re - im) * root, (re - im) * root)
                if sign > 0
                else ((im - re) * root, (-re - im) * root)
            )
        else:
            angle = 2.0 * math.pi * k / count
            cosine, sine = math.cos(angle), sign * math.sin(angle)
            re, im = re * cosine - im * sine, re * sine + im * cosine
        first.append((even[k][0] + re, even[k][1] + im))
        second.append((even[k][0] - re, even[k][1] - im))
    return first + second


def lane_slice(tile):
    return pl.ds(tile * LANES, LANES)


def weight_kernel(side, blocks_per_k, order, q_ref, owner_ref, mine_ref, other_ref, weight_ref):
    tiles = side * side // LANES
    lows = LANES // side
    scale = -1.0 / (NK * side**3)
    place, core = lax.axis_index("kb"), lax.axis_index("slab")
    line, column = place // 2, place % 2
    first_core = core == 0
    target_k = owner_ref[2 * line + core] // blocks_per_k
    lane = lax.broadcasted_iota(jnp.int32, (side, LANES), 1) // side
    for pair, d in enumerate(order):
        q = q_ref[target_k, owner_ref[2 * (line ^ d) + column] // blocks_per_k]
        mine, other = mine_ref[q], other_ref[q]
        low_half = jnp.where(first_core, mine, other) * scale
        high_half = jnp.where(first_core, other, mine) * scale
        for b in range(tiles):
            total = None
            for a in range(lows):
                row = a * tiles + b
                source, chunk = row // lows, row % lows
                half = low_half if source < tiles // 2 else high_half
                at = source % (tiles // 2) * LANES
                piece = half[:, at : at + LANES]
                shift = (a - chunk) % lows * side
                if shift:
                    piece = pltpu.roll(piece, shift, 1)
                total = piece if total is None else jnp.where(lane == a, piece, total)
            weight_ref[pair, :, lane_slice(b)] = total


def pair_kernel(side, count, first, has_sum, *refs):
    refs = list(refs)
    take = lambda n: [refs.pop(0) for _ in range(n)]
    own, beside = take(2), take(2)
    partners = [take(2) for _ in range(count)]
    (weight_ref,) = take(1)
    lane_f, lane_b, rows_f, rows_b, twist = take(5)
    sums = take(2) if has_sum else None
    outs = take(2)
    target, a_high, a_low, y_ref, f_high, f_low, g_ref = take(7)

    tiles = side * side // LANES
    half = side // 2
    rows = side * count

    def parts(ref):
        return ref[0], ref[1]

    home = lax.axis_index("kb") % 2 == lax.axis_index("slab")
    for h in range(2):
        target[h] = jnp.where(home, own[h][:, 0], beside[h][:, 0])
    for p in range(count):
        for h in range(2):
            row = p * side + h * half
            values = []
            for t in range(tiles):
                t_re, t_im = target[h, 0, :, lane_slice(t)], target[h, 1, :, lane_slice(t)]
                p_re = partners[p][h][0, 0, :, lane_slice(t)]
                p_im = partners[p][h][1, 0, :, lane_slice(t)]
                values.append((p_re * t_re + p_im * t_im, p_re * t_im - p_im * t_re))
            for b, (re, im) in enumerate(dft_list(values, -1)):
                if b:
                    cosine, sine = twist[b, 0], twist[b, 1]
                    re, im = re * cosine + im * sine, im * cosine - re * sine
                at = pl.ds(b * rows + row, half)
                for k, part in enumerate((re, im)):
                    high, low = split(part)
                    a_high[at, lane_slice(k)] = high
                    a_low[at, lane_slice(k)] = low
    y_ref[...] = dot_parts((a_high[...], a_low[...]), parts(lane_f))
    for n in range(tiles // 2):
        blocks = []
        for k in range(2):
            blocks.append(
                jnp.concatenate(
                    [y_ref[pl.ds((2 * n + j) * rows, rows), lane_slice(k)] for j in range(2)], 1
                )
            )
        spectrum = dot_parts(parts(rows_f), split(jnp.concatenate(blocks, 0)))
        weights = weight_ref[first : first + count, :, pl.ds(n * 2 * LANES, 2 * LANES)]
        weights = weights.reshape(rows, 2 * LANES)
        weighted = spectrum * jnp.concatenate([weights, weights], 0)
        back = dot_parts(parts(rows_b), split(weighted))
        high, low = split(back)
        for j in range(2):
            for k in range(2):
                at = (pl.ds((2 * n + j) * rows, rows), lane_slice(k))
                f_high[at] = high[k * rows : (k + 1) * rows, j * LANES : (j + 1) * LANES]
                f_low[at] = low[k * rows : (k + 1) * rows, j * LANES : (j + 1) * LANES]
    g_ref[...] = dot_parts((f_high[...], f_low[...]), parts(lane_b))
    gram_re = jnp.zeros((half, LANES), F32)
    gram_im = jnp.zeros((half, LANES), F32)
    for h in range(2):
        total = [[0.0, 0.0] for _ in range(tiles)]
        if has_sum:
            for t in range(tiles):
                total[t] = [sums[h][pl.ds((k * tiles + t) * half, half), :] for k in range(2)]
        for p in range(count):
            row = p * side + h * half
            values = []
            for b in range(tiles):
                at = pl.ds(b * rows + row, half)
                re, im = g_ref[at, lane_slice(0)], g_ref[at, lane_slice(1)]
                if b:
                    cosine, sine = twist[b, 0], twist[b, 1]
                    re, im = re * cosine - im * sine, im * cosine + re * sine
                values.append((re, im))
            for t, (re, im) in enumerate(dft_list(values, 1)):
                p_re = partners[p][h][0, 0, :, lane_slice(t)]
                p_im = partners[p][h][1, 0, :, lane_slice(t)]
                total[t][0] = total[t][0] + (p_re * re - p_im * im)
                total[t][1] = total[t][1] + (p_re * im + p_im * re)
        for t in range(tiles):
            re, im = total[t]
            t_re, t_im = target[h, 0, :, lane_slice(t)], target[h, 1, :, lane_slice(t)]
            gram_re += t_re * re + t_im * im
            gram_im += t_re * im - t_im * re
            outs[h][pl.ds(t * half, half), :] = re
            outs[h][pl.ds((tiles + t) * half, half), :] = im
    end = 2 * tiles * half
    scale = 1.0 / side**3
    sums_row = jnp.concatenate(
        [
            jnp.full((4, LANES), jnp.sum(gram_re) * scale, F32),
            jnp.full((4, LANES), jnp.sum(gram_im) * scale, F32),
        ],
        0,
    )
    for h in range(2):
        outs[h][pl.ds(end, 8), :] = sums_row


def join_kernel(own_ref, near_ref, away_ref, applied_ref, gram_ref):
    half = applied_ref.shape[2]
    tiles = applied_ref.shape[3] // LANES
    home = lax.axis_index("kb") % 2 == lax.axis_index("slab")
    for k in range(2):
        for t in range(tiles):
            at = pl.ds((k * tiles + t) * half, half)
            applied_ref[k, 0, :, lane_slice(t)] = (
                jnp.where(home, own_ref[at, :], near_ref[at, :]) + away_ref[at, :]
            )
    at = pl.ds(2 * tiles * half, 8)
    sums = jnp.where(home, own_ref[at, :], near_ref[at, :]) + away_ref[at, :]
    gram_ref[0, 0, 0] = jnp.max(sums[0:1, :])
    gram_ref[0, 0, 1] = jnp.max(sums[4:5, :])


VMEM = pl.BlockSpec(memory_space=pltpu.VMEM)
SMEM = pl.BlockSpec(memory_space=pltpu.SMEM)


COST = pl.CostEstimate(flops=2*10**10, bytes_accessed=10**8, transcendentals=0)


def params():
    return pltpu.CompilerParams(vmem_limit_bytes=48 * 2**20)


def choose_weights(q_index, owner, kernels, order, side, blocks_per_k):
    return pl.pallas_call(
        functools.partial(weight_kernel, side, blocks_per_k, order),
        out_shape=jax.ShapeDtypeStruct((len(order), side, side * side), F32),
        in_specs=[SMEM, SMEM, VMEM, VMEM],
        out_specs=VMEM,
        compiler_params=params(),
        cost_estimate=COST,
        name="weights",
    )(q_index, owner, *kernels)


def apply_pairs(own, beside, partners, weights, first, side, sums=None):
    count = len(partners)
    half = side // 2
    tiles = side * side // LANES
    rows = side * count
    lane = lane_table(side)
    across = sublane_table(side, count)
    tables = [
        jnp.asarray(bf16_parts(lane)),
        jnp.asarray(bf16_parts(lane.T)),
        jnp.asarray(bf16_parts(across)),
        jnp.asarray(bf16_parts(across.T)),
        jnp.asarray(twist_table(side, half)),
    ]
    operands = [*own, *beside] + [x for pair in partners for x in pair] + [weights] + tables
    operands += list(sums) if sums is not None else []
    message = jax.ShapeDtypeStruct((2 * tiles * half + 8, LANES), F32)
    return pl.pallas_call(
        functools.partial(pair_kernel, side, count, first, sums is not None),
        out_shape=(message, message),
        in_specs=[VMEM] * len(operands),
        out_specs=(VMEM, VMEM),
        scratch_shapes=[
            pltpu.VMEM((2, 2, half, side * side), F32),
            pltpu.VMEM((tiles * rows, 2 * LANES), BF16),
            pltpu.VMEM((tiles * rows, 2 * LANES), BF16),
            pltpu.VMEM((tiles * rows, 2 * LANES), F32),
            pltpu.VMEM((tiles * rows, 2 * LANES), BF16),
            pltpu.VMEM((tiles * rows, 2 * LANES), BF16),
            pltpu.VMEM((tiles * rows, 2 * LANES), F32),
        ],
        compiler_params=params(),
        cost_estimate=COST,
        name="pairs",
    )(*operands)


def join(own, near, away, shape):
    applied, gram = pl.pallas_call(
        join_kernel,
        out_shape=(jax.ShapeDtypeStruct(shape, F32), jax.ShapeDtypeStruct((1, 1, 2), F32)),
        in_specs=[VMEM, VMEM, VMEM],
        out_specs=(VMEM, SMEM),
        compiler_params=params(),
        cost_estimate=COST,
        name="join",
    )(own, near, away)
    return applied, gram.transpose(2, 0, 1)


def block_gram(orbitals, applied, owner, blocks_per_k, cells):
    highest = lax.Precision.HIGHEST
    partners = lax.all_gather(orbitals, "kb", axis=1, tiled=True)
    re = jnp.einsum("pxa,txa->tp", partners[0], applied[0], precision=highest)
    re += jnp.einsum("pxa,txa->tp", partners[1], applied[1], precision=highest)
    im = jnp.einsum("pxa,txa->tp", partners[0], applied[1], precision=highest)
    im -= jnp.einsum("pxa,txa->tp", partners[1], applied[0], precision=highest)
    sums = lax.psum(jnp.stack([re, im]) / cells, "slab")
    own = owner[lax.axis_index("kb")] // blocks_per_k
    wanted = own * blocks_per_k + jnp.arange(blocks_per_k, dtype=jnp.int32)
    selector = jnp.where(owner[:, None] == wanted[None], 1.0, 0.0).astype(F32)
    return jnp.einsum("ktp,pc->ktc", sums, selector, precision=highest)


def on_device(orbitals, kernel, q_index, owner):
    side = kernel.shape[1]
    n_kb = lax.axis_size("kb")
    lines = n_kb // 2
    blocks_per_k = n_kb // NK
    place, core = lax.axis_index("kb"), lax.axis_index("slab")
    column = place % 2
    across = [(a, a ^ 1) for a in range(n_kb)]

    def swap(x):
        return lax.ppermute(x, "slab", [(0, 1), (1, 0)])

    def from_line(x, d):
        return lax.ppermute(
            x, "kb", [(2 * a + c, 2 * (a ^ d) + c) for a in range(lines) for c in range(2)]
        )

    order = list(range(lines))
    arrived = {d: from_line(orbitals, d) for d in [*order[2:], 1]}
    beside = lax.ppermute(orbitals, "kb", across)
    far_kernel = swap(kernel)
    weights = choose_weights(
        q_index, owner, (kernel, far_kernel), tuple(order), side, blocks_per_k
    )
    own = (orbitals, swap(lax.optimization_barrier((orbitals, far_kernel))[0]))
    arrived[2], weights = lax.optimization_barrier((arrived[2], weights))
    arrived[1], beside, arrived[2] = lax.optimization_barrier((arrived[1], beside, arrived[2]))
    beside = (beside, swap(beside))
    partners = [own] + [(arrived[d], swap(arrived[d])) for d in order[1:]]
    sums = None
    for at in range(0, lines, 4):
        sums = apply_pairs(own, beside, partners[at : at + 4], weights, at, side, sums)
    mine, far = sums
    near = swap(far)
    away = lax.ppermute(jnp.where(core == column, near, mine), "kb", across)
    applied, gram = join(mine, near, away, orbitals.shape)
    if blocks_per_k > 1:
        gram = block_gram(orbitals, applied, owner, blocks_per_k, side**3)
    return applied, gram


def solution(mesh):
    in_specs = (P(None, ("grp", "kb"), "slab", None), P(None, None, "slab"), P(), P())
    out_specs = (P(None, ("grp", "kb"), "slab", None), P(None, ("grp", "kb"), None))
    return jax.shard_map(
        on_device, mesh=mesh, in_specs=in_specs, out_specs=out_specs, check_vma=False
    )
```

```python
import functools
import math

import jax
import jax.numpy as jnp
import numpy as np
from jax import lax
from jax.experimental import pallas as pl
from jax.experimental.pallas import tpu as pltpu
from jax.sharding import PartitionSpec as P

NK = 8
GROUP = 4
LANES = 128
F32 = jnp.float32
BF16 = jnp.bfloat16


def bf16_parts(table):
    high = table.astype(np.float32).astype(BF16)
    low = (table - high.astype(np.float64)).astype(np.float32).astype(BF16)
    return np.stack([high, low])


def lane_table(side):
    lows = LANES // side
    index = np.arange(LANES)
    low, z = index // side, index % side
    phase = 2.0 * math.pi * (np.outer(low, low) / lows + np.outer(z, z) / side)
    real, imag = np.cos(phase), -np.sin(phase)
    return np.block([[real, imag], [-imag, real]])


def turn_table(side):
    phase = 2.0 * math.pi * np.outer(np.arange(side // 2), np.arange(2 * GROUP) // GROUP) / side
    both = np.stack([np.cos(phase), np.sin(phase)], 1).astype(np.float32)
    return np.ascontiguousarray(np.broadcast_to(both[..., None], (*both.shape, LANES)))


def twist_table(side, rows):
    tiles = side * side // LANES
    phase = 2.0 * math.pi * np.outer(np.arange(tiles), np.arange(LANES) // side) / side
    both = np.stack([np.cos(phase), np.sin(phase)], 1).astype(np.float32)
    return np.ascontiguousarray(np.broadcast_to(both[:, :, None], (tiles, 2, rows, LANES)))


def split(value):
    high = value.astype(BF16)
    return high, (value - high.astype(F32)).astype(BF16)


def dot_parts(left, right):
    dot = functools.partial(jnp.dot, preferred_element_type=F32)
    return dot(left[0], right[0]) + (dot(left[1], right[0]) + dot(left[0], right[1]))


def dft_list(values, sign):
    count = len(values)
    if count == 1:
        return values
    even, odd = dft_list(values[0::2], sign), dft_list(values[1::2], sign)
    first, second = [], []
    for k in range(count // 2):
        re, im = odd[k]
        eighth = 8 * k // count if 8 * k % count == 0 else None
        if eighth == 0:
            pass
        elif eighth == 2:
            re, im = (-im, re) if sign > 0 else (im, -re)
        elif eighth == 1:
            root = math.sqrt(0.5)
            re, im = (
                ((re - im) * root, (re + im) * root)
                if sign > 0
                else ((re + im) * root, (im - re) * root)
            )
        elif eighth == 3:
            root = math.sqrt(0.5)
            re, im = (
                ((-re - im) * root, (re - im) * root)
                if sign > 0
                else ((im - re) * root, (-re - im) * root)
            )
        else:
            angle = 2.0 * math.pi * k / count
            cosine, sine = math.cos(angle), sign * math.sin(angle)
            re, im = re * cosine - im * sine, re * sine + im * cosine
        first.append((even[k][0] + re, even[k][1] + im))
        second.append((even[k][0] - re, even[k][1] - im))
    return first + second


def lane_slice(tile):
    return pl.ds(tile * LANES, LANES)


def weight_kernel(side, blocks_per_k, order, q_ref, owner_ref, mine_ref, other_ref, weight_ref):
    tiles = side * side // LANES
    lows = LANES // side
    scale = -1.0 / (NK * side**3)
    place, core = lax.axis_index("kb"), lax.axis_index("slab")
    line, column = place // 2, place % 2
    first_core = core == 0
    target_k = owner_ref[2 * line + core] // blocks_per_k
    lane = lax.broadcasted_iota(jnp.int32, (side, LANES), 1) // side
    for pair, d in enumerate(order):
        q = q_ref[target_k, owner_ref[2 * (line ^ d) + column] // blocks_per_k]
        mine, other = mine_ref[q], other_ref[q]
        low_half = jnp.where(first_core, mine, other) * scale
        high_half = jnp.where(first_core, other, mine) * scale
        for b in range(tiles):
            total = None
            for a in range(lows):
                row = a * tiles + b
                source, chunk = row // lows, row % lows
                half = low_half if source < tiles // 2 else high_half
                at = source % (tiles // 2) * LANES
                piece = half[:, at : at + LANES]
                shift = (a - chunk) % lows * side
                if shift:
                    piece = pltpu.roll(piece, shift, 1)
                total = piece if total is None else jnp.where(lane == a, piece, total)
            at = pl.ds(b * GROUP * side + pair % GROUP, side, stride=GROUP)
            weight_ref[pair // GROUP, at, :] = total


def pair_kernel(side, at_group, has_sum, *refs):
    refs = list(refs)
    take = lambda n: [refs.pop(0) for _ in range(n)]
    partners = [take(2) for _ in range(GROUP)]
    own, beside = take(2), take(2)
    (weight_ref,) = take(1)
    lane_f, lane_b, twist, turn = take(4)
    sums = take(2) if has_sum else None
    outs = take(2)
    target, x_re, x_im, high_ref, low_ref, g_ref = take(6)

    tiles = side * side // LANES
    half = side // 2
    subs = 2 * GROUP
    rows = half * subs

    def parts(ref):
        return ref[0], ref[1]

    sign = jnp.where(lax.broadcasted_iota(jnp.int32, (subs, LANES), 0) < GROUP, 1.0, -1.0)

    def halves(value):
        return pltpu.roll(value, GROUP, 0) + value * sign

    home = lax.axis_index("kb") % 2 == lax.axis_index("slab")
    for h in range(2):
        target[h] = jnp.where(home, own[h][:, 0], beside[h][:, 0])

    for p in range(GROUP):
        for h in range(2):
            values = []
            for t in range(tiles):
                t_re, t_im = target[h, 0, :, lane_slice(t)], target[h, 1, :, lane_slice(t)]
                p_re = partners[p][h][0, 0, :, lane_slice(t)]
                p_im = partners[p][h][1, 0, :, lane_slice(t)]
                values.append((p_re * t_re + p_im * t_im, p_re * t_im - p_im * t_re))
            for b, (re, im) in enumerate(dft_list(values, -1)):
                if b:
                    cosine, sine = twist[b, 0], twist[b, 1]
                    re, im = re * cosine + im * sine, im * cosine - re * sine
                at = pl.ds(b * rows + h * GROUP + p, half, stride=subs)
                x_re[at, :] = re
                x_im[at, :] = im
    def forward(b):
        values = []
        for x in range(half):
            at = pl.ds(b * rows + x * subs, subs)
            re, im = halves(x_re[at, :]), halves(x_im[at, :])
            if x:
                cosine, sine = turn[x, 0], turn[x, 1]
                re, im = re * cosine + im * sine, im * cosine - re * sine
            values.append((re, im))
        values = dft_list(values, -1)
        for x in range(0, half, 2):
            at = pl.ds(b * rows + x * subs, 2 * subs)
            for k in range(2):
                high, low = split(jnp.concatenate([values[x][k], values[x + 1][k]], 0))
                high_ref[at, lane_slice(k)] = high
                low_ref[at, lane_slice(k)] = low

    def middle(b):
        at = pl.ds(b * rows, rows)
        spectrum = dot_parts((high_ref[at, :], low_ref[at, :]), parts(lane_f))
        weights = weight_ref[at_group, at, :]
        weighted = split(spectrum * jnp.concatenate([weights, weights], 1))
        g_ref[at, :] = dot_parts(weighted, parts(lane_b))

    def backward(b):
        values = []
        for x in range(half):
            at = pl.ds(b * rows + x * subs, subs)
            values.append((g_ref[at, lane_slice(0)], g_ref[at, lane_slice(1)]))
        for x, (re, im) in enumerate(dft_list(values, 1)):
            if x:
                cosine, sine = turn[x, 0], turn[x, 1]
                re, im = re * cosine - im * sine, im * cosine + re * sine
            at = pl.ds(b * rows + x * subs, subs)
            x_re[at, :] = halves(re)
            x_im[at, :] = halves(im)

    for b in range(tiles):
        forward(b)
        middle(b)
        backward(b)
    gram_re = jnp.zeros((half, LANES), F32)
    gram_im = jnp.zeros((half, LANES), F32)
    for h in range(2):
        total = [[0.0, 0.0] for _ in range(tiles)]
        if has_sum:
            for t in range(tiles):
                total[t] = [sums[h][pl.ds((k * tiles + t) * half, half), :] for k in range(2)]
        for p in range(GROUP):
            values = []
            for b in range(tiles):
                at = pl.ds(b * rows + h * GROUP + p, half, stride=subs)
                re, im = x_re[at, :], x_im[at, :]
                if b:
                    cosine, sine = twist[b, 0], twist[b, 1]
                    re, im = re * cosine - im * sine, im * cosine + re * sine
                values.append((re, im))
            for t, (re, im) in enumerate(dft_list(values, 1)):
                p_re = partners[p][h][0, 0, :, lane_slice(t)]
                p_im = partners[p][h][1, 0, :, lane_slice(t)]
                total[t][0] = total[t][0] + (p_re * re - p_im * im)
                total[t][1] = total[t][1] + (p_re * im + p_im * re)
        for t in range(tiles):
            re, im = total[t]
            t_re, t_im = target[h, 0, :, lane_slice(t)], target[h, 1, :, lane_slice(t)]
            gram_re += t_re * re + t_im * im
            gram_im += t_re * im - t_im * re
            outs[h][pl.ds(t * half, half), :] = re
            outs[h][pl.ds((tiles + t) * half, half), :] = im
    end = 2 * tiles * half
    scale = 1.0 / side**3
    sums_row = jnp.concatenate(
        [
            jnp.full((4, LANES), jnp.sum(gram_re) * scale, F32),
            jnp.full((4, LANES), jnp.sum(gram_im) * scale, F32),
        ],
        0,
    )
    for h in range(2):
        outs[h][pl.ds(end, 8), :] = sums_row


def join_kernel(own_ref, near_ref, away_ref, applied_ref, gram_ref):
    half = applied_ref.shape[2]
    tiles = applied_ref.shape[3] // LANES
    home = lax.axis_index("kb") % 2 == lax.axis_index("slab")
    for k in range(2):
        for t in range(tiles):
            at = pl.ds((k * tiles + t) * half, half)
            applied_ref[k, 0, :, lane_slice(t)] = (
                jnp.where(home, own_ref[at, :], near_ref[at, :]) + away_ref[at, :]
            )
    at = pl.ds(2 * tiles * half, 8)
    sums = jnp.where(home, own_ref[at, :], near_ref[at, :]) + away_ref[at, :]
    gram_ref[0, 0, 0] = jnp.max(sums[0:1, :])
    gram_ref[0, 0, 1] = jnp.max(sums[4:5, :])


VMEM = pl.BlockSpec(memory_space=pltpu.VMEM)
SMEM = pl.BlockSpec(memory_space=pltpu.SMEM)


COST = pl.CostEstimate(flops=2*10**10, bytes_accessed=10**8, transcendentals=0)


def params():
    return pltpu.CompilerParams(vmem_limit_bytes=48 * 2**20)


def choose_weights(q_index, owner, kernels, order, side, blocks_per_k):
    return pl.pallas_call(
        functools.partial(weight_kernel, side, blocks_per_k, order),
        out_shape=jax.ShapeDtypeStruct((len(order) // GROUP, GROUP * side**3 // LANES, LANES), F32),
        in_specs=[SMEM, SMEM, VMEM, VMEM],
        out_specs=VMEM,
        compiler_params=params(),
        cost_estimate=COST,
        name="weights",
    )(q_index, owner, *kernels)


def apply_pairs(own, beside, partners, weights, at_group, side, sums=None):
    half = side // 2
    tiles = side * side // LANES
    rows = tiles * half * 2 * GROUP
    lane = lane_table(side)
    tables = [
        jnp.asarray(bf16_parts(lane)),
        jnp.asarray(bf16_parts(lane.T)),
        jnp.asarray(twist_table(side, half)),
        jnp.asarray(turn_table(side)),
    ]
    operands = [x for pair in partners for x in pair] + [*own, *beside, weights] + tables
    operands += list(sums) if sums is not None else []
    message = jax.ShapeDtypeStruct((2 * tiles * half + 8, LANES), F32)
    return pl.pallas_call(
        functools.partial(pair_kernel, side, at_group, sums is not None),
        out_shape=(message, message),
        in_specs=[VMEM] * len(operands),
        out_specs=(VMEM, VMEM),
        scratch_shapes=[
            pltpu.VMEM((2, 2, half, side * side), F32),
            pltpu.VMEM((rows, LANES), F32),
            pltpu.VMEM((rows, LANES), F32),
            pltpu.VMEM((rows, 2 * LANES), BF16),
            pltpu.VMEM((rows, 2 * LANES), BF16),
            pltpu.VMEM((rows, 2 * LANES), F32),
        ],
        compiler_params=params(),
        cost_estimate=COST,
        name="pairs",
    )(*operands)


def join(own, near, away, shape):
    applied, gram = pl.pallas_call(
        join_kernel,
        out_shape=(jax.ShapeDtypeStruct(shape, F32), jax.ShapeDtypeStruct((1, 1, 2), F32)),
        in_specs=[VMEM, VMEM, VMEM],
        out_specs=(VMEM, SMEM),
        compiler_params=params(),
        cost_estimate=COST,
        name="join",
    )(own, near, away)
    return applied, gram.transpose(2, 0, 1)


def block_gram(orbitals, applied, owner, blocks_per_k, cells):
    highest = lax.Precision.HIGHEST
    partners = lax.all_gather(orbitals, "kb", axis=1, tiled=True)
    re = jnp.einsum("pxa,txa->tp", partners[0], applied[0], precision=highest)
    re += jnp.einsum("pxa,txa->tp", partners[1], applied[1], precision=highest)
    im = jnp.einsum("pxa,txa->tp", partners[0], applied[1], precision=highest)
    im -= jnp.einsum("pxa,txa->tp", partners[1], applied[0], precision=highest)
    sums = lax.psum(jnp.stack([re, im]) / cells, "slab")
    own = owner[lax.axis_index("kb")] // blocks_per_k
    wanted = own * blocks_per_k + jnp.arange(blocks_per_k, dtype=jnp.int32)
    selector = jnp.where(owner[:, None] == wanted[None], 1.0, 0.0).astype(F32)
    return jnp.einsum("ktp,pc->ktc", sums, selector, precision=highest)


def on_device(orbitals, kernel, q_index, owner):
    side = kernel.shape[1]
    n_kb = lax.axis_size("kb")
    lines = n_kb // 2
    blocks_per_k = n_kb // NK
    place, core = lax.axis_index("kb"), lax.axis_index("slab")
    column = place % 2
    across = [(a, a ^ 1) for a in range(n_kb)]

    def swap(x):
        return lax.ppermute(x, "slab", [(0, 1), (1, 0)])

    def from_line(x, d):
        return lax.ppermute(
            x, "kb", [(2 * a + c, 2 * (a ^ d) + c) for a in range(lines) for c in range(2)]
        )

    order = [*range(2, lines), 1, 0]
    arrived = {d: from_line(orbitals, d) for d in order[:-1]}
    beside = lax.ppermute(orbitals, "kb", across)
    far_kernel = swap(kernel)
    weights = choose_weights(
        q_index, owner, (kernel, far_kernel), tuple(order), side, blocks_per_k
    )
    own_far = swap(lax.optimization_barrier((orbitals, far_kernel))[0])
    names = (*order[:-1], 0)
    landed = lax.optimization_barrier(tuple(arrived[d] if d else beside for d in names) + (own_far, weights))
    arrived = dict(zip(names, landed))
    beside, weights = arrived[0], landed[-1]
    own = (orbitals, landed[-2])
    beside = (beside, swap(beside))
    partners = [(arrived[d], swap(arrived[d])) for d in order[:-1]] + [own]
    sums = None
    for at in range(0, lines, GROUP):
        sums = apply_pairs(own, beside, partners[at : at + GROUP], weights, at // GROUP, side, sums)
    mine, far = sums
    near = swap(far)
    away = lax.ppermute(jnp.where(core == column, near, mine), "kb", across)
    applied, gram = join(mine, near, away, orbitals.shape)
    if blocks_per_k > 1:
        gram = block_gram(orbitals, applied, owner, blocks_per_k, side**3)
    return applied, gram


def solution(mesh):
    in_specs = (P(None, ("grp", "kb"), "slab", None), P(None, None, "slab"), P(), P())
    out_specs = (P(None, ("grp", "kb"), "slab", None), P(None, ("grp", "kb"), None))
    return jax.shard_map(
        on_device, mesh=mesh, in_specs=in_specs, out_specs=out_specs, check_vma=False
    )
```

```python
import functools
import math

import jax
import jax.numpy as jnp
import numpy as np
from jax import lax
from jax.experimental import pallas as pl
from jax.experimental.pallas import tpu as pltpu
from jax.sharding import PartitionSpec as P

NK = 8
SUBLANES = 8
STEP = 9
GROUP = 4
LANES = 128
F32 = jnp.float32
BF16 = jnp.bfloat16


def bf16_parts(table):
    high = table.astype(np.float32).astype(BF16)
    low = (table - high.astype(np.float64)).astype(np.float32).astype(BF16)
    return np.stack([high, low])


def lane_table(side):
    lows = LANES // side
    index = np.arange(LANES)
    low, z = index // side, index % side
    phase = 2.0 * math.pi * (np.outer(low, low) / lows + np.outer(z, z) / side)
    real, imag = np.cos(phase), -np.sin(phase)
    return np.block([[real, imag], [-imag, real]])


def turn_table(side):
    phase = 2.0 * math.pi * np.arange(side // 2) / side
    both = np.stack([np.cos(phase), np.sin(phase)]).astype(np.float32)
    return np.ascontiguousarray(np.broadcast_to(both[..., None], (*both.shape, LANES)))


def twist_table(side, rows):
    tiles = side * side // LANES
    phase = 2.0 * math.pi * np.outer(np.arange(tiles), np.arange(LANES) // side) / side
    both = np.stack([np.cos(phase), np.sin(phase)], 1).astype(np.float32)
    return np.ascontiguousarray(np.broadcast_to(both[:, :, None], (tiles, 2, rows, LANES)))


def split(value):
    high = value.astype(BF16)
    return high, (value - high.astype(F32)).astype(BF16)


def dot_parts(left, right):
    dot = functools.partial(jnp.dot, preferred_element_type=F32)
    return dot(left[0], right[0]) + (dot(left[1], right[0]) + dot(left[0], right[1]))


def dft_list(values, sign):
    count = len(values)
    if count == 1:
        return values
    even, odd = dft_list(values[0::2], sign), dft_list(values[1::2], sign)
    first, second = [], []
    for k in range(count // 2):
        re, im = odd[k]
        eighth = 8 * k // count if 8 * k % count == 0 else None
        if eighth == 0:
            pass
        elif eighth == 2:
            re, im = (-im, re) if sign > 0 else (im, -re)
        elif eighth == 1:
            root = math.sqrt(0.5)
            re, im = (
                ((re - im) * root, (re + im) * root)
                if sign > 0
                else ((re + im) * root, (im - re) * root)
            )
        elif eighth == 3:
            root = math.sqrt(0.5)
            re, im = (
                ((-re - im) * root, (re - im) * root)
                if sign > 0
                else ((im - re) * root, (-re - im) * root)
            )
        else:
            angle = 2.0 * math.pi * k / count
            cosine, sine = math.cos(angle), sign * math.sin(angle)
            re, im = re * cosine - im * sine, re * sine + im * cosine
        first.append((even[k][0] + re, even[k][1] + im))
        second.append((even[k][0] - re, even[k][1] - im))
    return first + second


def lane_slice(tile):
    return pl.ds(tile * LANES, LANES)


def weight_kernel(side, blocks_per_k, order, q_ref, owner_ref, mine_ref, other_ref, weight_ref):
    tiles = side * side // LANES
    lows = LANES // side
    scale = -1.0 / (NK * side**3)
    place, core = lax.axis_index("kb"), lax.axis_index("slab")
    line, column = place // 2, place % 2
    first_core = core == 0
    target_k = owner_ref[2 * line + core] // blocks_per_k
    lane = lax.broadcasted_iota(jnp.int32, (side, LANES), 1) // side
    for pair, d in enumerate(order):
        q = q_ref[target_k, owner_ref[2 * (line ^ d) + column] // blocks_per_k]
        mine, other = mine_ref[q], other_ref[q]
        low_half = jnp.where(first_core, mine, other) * scale
        high_half = jnp.where(first_core, other, mine) * scale
        for b in range(tiles):
            total = None
            for a in range(lows):
                row = a * tiles + b
                source, chunk = row // lows, row % lows
                half = low_half if source < tiles // 2 else high_half
                at = source % (tiles // 2) * LANES
                piece = half[:, at : at + LANES]
                shift = (a - chunk) % lows * side
                if shift:
                    piece = pltpu.roll(piece, shift, 1)
                total = piece if total is None else jnp.where(lane == a, piece, total)
            at = pl.ds(b // GROUP * GROUP * side + b % GROUP, side, stride=GROUP)
            weight_ref[pair, at, :] = total


def pair_kernel(side, count, first, has_sum, *refs):
    refs = list(refs)
    take = lambda n: [refs.pop(0) for _ in range(n)]
    partners = [take(2) for _ in range(count)]
    own, beside = take(2), take(2)
    (weight_ref,) = take(1)
    lane_f, lane_b, twist, turn = take(4)
    sums = take(2) if has_sum else None
    outs = take(2)
    target, x_re, x_im, high_ref, low_ref, g_ref = take(6)

    tiles = side * side // LANES
    half = side // 2
    subs = 2 * GROUP
    rows = half * subs

    def parts(ref):
        return ref[0], ref[1]

    home = lax.axis_index("kb") % 2 == lax.axis_index("slab")
    for h in range(2):
        target[h] = jnp.where(home, own[h][:, 0], beside[h][:, 0])

    groups = tiles // GROUP

    def spread(p, b, x, parity):
        start = ((p * groups + b // GROUP) * half + x) * STEP + parity * GROUP + b % GROUP
        return pl.ds(start, SUBLANES, stride=STEP)

    def packed(g, x):
        return pl.ds((g * half + x) * STEP, subs)

    def densities(p):
        for x in range(0, half, SUBLANES):
            block = pl.ds(x, SUBLANES)
            both = []
            for h in range(2):
                values = []
                for t in range(tiles):
                    t_re, t_im = target[h, 0, block, lane_slice(t)], target[h, 1, block, lane_slice(t)]
                    p_re = partners[p][h][0, 0, block, lane_slice(t)]
                    p_im = partners[p][h][1, 0, block, lane_slice(t)]
                    values.append((p_re * t_re + p_im * t_im, p_re * t_im - p_im * t_re))
                both.append(dft_list(values, -1))
            turn_re, turn_im = turn[0, block], turn[1, block]
            for b in range(tiles):
                (re_0, im_0), (re_1, im_1) = both[0][b], both[1][b]
                re, im = re_0 - re_1, im_0 - im_1
                even = re_0 + re_1, im_0 + im_1
                odd = re * turn_re + im * turn_im, im * turn_re - re * turn_im
                for parity, (re, im) in enumerate((even, odd)):
                    if b:
                        cosine, sine = twist[b, 0], twist[b, 1]
                        re, im = re * cosine + im * sine, im * cosine - re * sine
                    x_re[spread(p, b, x, parity), :] = re
                    x_im[spread(p, b, x, parity), :] = im

    def forward(g):
        values = [(x_re[packed(g, x), :], x_im[packed(g, x), :]) for x in range(half)]
        values = dft_list(values, -1)
        for x in range(0, half, 2):
            at = pl.ds(g * rows + x * subs, 2 * subs)
            for k in range(2):
                high, low = split(jnp.concatenate([values[x][k], values[x + 1][k]], 0))
                high_ref[at, lane_slice(k)] = high
                low_ref[at, lane_slice(k)] = low

    def middle(g):
        at = pl.ds(g * rows, rows)
        spectrum = dot_parts((high_ref[at, :], low_ref[at, :]), parts(lane_f))
        weights = weight_ref[first + g // groups, pl.ds(g % groups * rows, rows), :]
        weighted = split(spectrum * jnp.concatenate([weights, weights], 1))
        g_ref[at, :] = dot_parts(weighted, parts(lane_b))

    def backward(g):
        values = []
        for x in range(half):
            at = pl.ds(g * rows + x * subs, subs)
            values.append((g_ref[at, lane_slice(0)], g_ref[at, lane_slice(1)]))
        for x, (re, im) in enumerate(dft_list(values, 1)):
            x_re[packed(g, x), :] = re
            x_im[packed(g, x), :] = im

    for p in range(count):
        densities(p)
        for g in range(p * groups, (p + 1) * groups):
            forward(g)
            middle(g)
            backward(g)
    gram_re = jnp.zeros((SUBLANES, LANES), F32)
    gram_im = jnp.zeros((SUBLANES, LANES), F32)
    for x in range(0, half, SUBLANES):
        block = pl.ds(x, SUBLANES)
        total = [[[0.0, 0.0] for _ in range(tiles)] for _ in range(2)]
        if has_sum:
            for h in range(2):
                for t in range(tiles):
                    for k in range(2):
                        total[h][t][k] = sums[h][pl.ds((k * tiles + t) * half + x, SUBLANES), :]
        turn_re, turn_im = turn[0, block], turn[1, block]
        for p in range(count):
            both = [], []
            for b in range(tiles):
                pair = []
                for parity in range(2):
                    re, im = x_re[spread(p, b, x, parity), :], x_im[spread(p, b, x, parity), :]
                    if b:
                        cosine, sine = twist[b, 0], twist[b, 1]
                        re, im = re * cosine - im * sine, im * cosine + re * sine
                    pair.append((re, im))
                re, im = pair[1]
                re, im = re * turn_re - im * turn_im, im * turn_re + re * turn_im
                both[0].append((pair[0][0] + re, pair[0][1] + im))
                both[1].append((pair[0][0] - re, pair[0][1] - im))
            for h in range(2):
                for t, (re, im) in enumerate(dft_list(both[h], 1)):
                    p_re = partners[p][h][0, 0, block, lane_slice(t)]
                    p_im = partners[p][h][1, 0, block, lane_slice(t)]
                    total[h][t][0] = total[h][t][0] + (p_re * re - p_im * im)
                    total[h][t][1] = total[h][t][1] + (p_re * im + p_im * re)
        for h in range(2):
            for t in range(tiles):
                re, im = total[h][t]
                t_re, t_im = target[h, 0, block, lane_slice(t)], target[h, 1, block, lane_slice(t)]
                gram_re += t_re * re + t_im * im
                gram_im += t_re * im - t_im * re
                outs[h][pl.ds(t * half + x, SUBLANES), :] = re
                outs[h][pl.ds((tiles + t) * half + x, SUBLANES), :] = im
    end = 2 * tiles * half
    scale = 1.0 / side**3
    sums_row = jnp.concatenate(
        [
            jnp.full((4, LANES), jnp.sum(gram_re) * scale, F32),
            jnp.full((4, LANES), jnp.sum(gram_im) * scale, F32),
        ],
        0,
    )
    for h in range(2):
        outs[h][pl.ds(end, 8), :] = sums_row


def join_kernel(own_ref, near_ref, away_ref, applied_ref, gram_ref):
    half = applied_ref.shape[2]
    tiles = applied_ref.shape[3] // LANES
    home = lax.axis_index("kb") % 2 == lax.axis_index("slab")
    for k in range(2):
        for t in range(tiles):
            at = pl.ds((k * tiles + t) * half, half)
            applied_ref[k, 0, :, lane_slice(t)] = (
                jnp.where(home, own_ref[at, :], near_ref[at, :]) + away_ref[at, :]
            )
    at = pl.ds(2 * tiles * half, 8)
    sums = jnp.where(home, own_ref[at, :], near_ref[at, :]) + away_ref[at, :]
    gram_ref[0, 0, 0] = jnp.max(sums[0:1, :])
    gram_ref[0, 0, 1] = jnp.max(sums[4:5, :])


VMEM = pl.BlockSpec(memory_space=pltpu.VMEM)
SMEM = pl.BlockSpec(memory_space=pltpu.SMEM)


COST = pl.CostEstimate(flops=2*10**10, bytes_accessed=10**8, transcendentals=0)


def params():
    return pltpu.CompilerParams(vmem_limit_bytes=48 * 2**20)


def choose_weights(q_index, owner, kernels, order, side, blocks_per_k):
    return pl.pallas_call(
        functools.partial(weight_kernel, side, blocks_per_k, order),
        out_shape=jax.ShapeDtypeStruct((len(order), side**3 // LANES, LANES), F32),
        in_specs=[SMEM, SMEM, VMEM, VMEM],
        out_specs=VMEM,
        compiler_params=params(),
        cost_estimate=COST,
        name="weights",
    )(q_index, owner, *kernels)


def apply_pairs(own, beside, partners, weights, first, side, sums=None):
    count = len(partners)
    half = side // 2
    tiles = side * side // LANES
    rows = count * side**3 // LANES
    lane = lane_table(side)
    tables = [
        jnp.asarray(bf16_parts(lane)),
        jnp.asarray(bf16_parts(lane.T)),
        jnp.asarray(twist_table(side, SUBLANES)),
        jnp.asarray(turn_table(side)),
    ]
    operands = [x for pair in partners for x in pair] + [*own, *beside, weights] + tables
    operands += list(sums) if sums is not None else []
    message = jax.ShapeDtypeStruct((2 * tiles * half + 8, LANES), F32)
    return pl.pallas_call(
        functools.partial(pair_kernel, side, count, first, sums is not None),
        out_shape=(message, message),
        in_specs=[VMEM] * len(operands),
        out_specs=(VMEM, VMEM),
        scratch_shapes=[
            pltpu.VMEM((2, 2, half, side * side), F32),
            pltpu.VMEM((rows // SUBLANES * STEP, LANES), F32),
            pltpu.VMEM((rows // SUBLANES * STEP, LANES), F32),
            pltpu.VMEM((rows, 2 * LANES), BF16),
            pltpu.VMEM((rows, 2 * LANES), BF16),
            pltpu.VMEM((rows, 2 * LANES), F32),
        ],
        compiler_params=params(),
        cost_estimate=COST,
        name="pairs",
    )(*operands)


def join(own, near, away, shape):
    applied, gram = pl.pallas_call(
        join_kernel,
        out_shape=(jax.ShapeDtypeStruct(shape, F32), jax.ShapeDtypeStruct((1, 1, 2), F32)),
        in_specs=[VMEM, VMEM, VMEM],
        out_specs=(VMEM, SMEM),
        compiler_params=params(),
        cost_estimate=COST,
        name="join",
    )(own, near, away)
    return applied, gram.transpose(2, 0, 1)


def block_gram(orbitals, applied, owner, blocks_per_k, cells):
    highest = lax.Precision.HIGHEST
    partners = lax.all_gather(orbitals, "kb", axis=1, tiled=True)
    re = jnp.einsum("pxa,txa->tp", partners[0], applied[0], precision=highest)
    re += jnp.einsum("pxa,txa->tp", partners[1], applied[1], precision=highest)
    im = jnp.einsum("pxa,txa->tp", partners[0], applied[1], precision=highest)
    im -= jnp.einsum("pxa,txa->tp", partners[1], applied[0], precision=highest)
    sums = lax.psum(jnp.stack([re, im]) / cells, "slab")
    own = owner[lax.axis_index("kb")] // blocks_per_k
    wanted = own * blocks_per_k + jnp.arange(blocks_per_k, dtype=jnp.int32)
    selector = jnp.where(owner[:, None] == wanted[None], 1.0, 0.0).astype(F32)
    return jnp.einsum("ktp,pc->ktc", sums, selector, precision=highest)


def on_device(orbitals, kernel, q_index, owner):
    side = kernel.shape[1]
    n_kb = lax.axis_size("kb")
    lines = n_kb // 2
    blocks_per_k = n_kb // NK
    place, core = lax.axis_index("kb"), lax.axis_index("slab")
    column = place % 2
    across = [(a, a ^ 1) for a in range(n_kb)]

    def swap(x):
        return lax.ppermute(x, "slab", [(0, 1), (1, 0)])

    def from_line(x, d):
        return lax.ppermute(
            x, "kb", [(2 * a + c, 2 * (a ^ d) + c) for a in range(lines) for c in range(2)]
        )

    order = [0, 1, *range(2, lines)]
    first = [2, 1, 0]
    last = [d for d in order if d and d not in first]
    arrived = {d: from_line(orbitals, d) for d in order[1:]}
    arrived[0] = lax.ppermute(orbitals, "kb", across)
    far_kernel = swap(kernel)
    weights = choose_weights(
        q_index, owner, (kernel, far_kernel), tuple(order), side, blocks_per_k
    )
    own_far = swap(lax.optimization_barrier((orbitals, far_kernel))[0])
    landed = lax.optimization_barrier((*(arrived[d] for d in first), weights))
    arrived.update(zip(first, landed))
    weights = landed[-1]
    far = {d: swap(arrived[d]) for d in first}
    landed = lax.optimization_barrier(
        (*(arrived[d] for d in last), *(far[d] for d in first), own_far)
    )
    arrived.update(zip(last, landed))
    far.update(zip(first, landed[len(last) :]))
    own = (orbitals, landed[-1])
    far.update({d: swap(arrived[d]) for d in last})
    beside = (arrived[0], far[0])
    partners = [own] + [(arrived[d], far[d]) for d in order[1:]]
    if lines <= 4:
        groups = [(0, lines - 1), (lines - 1, lines)]
    else:
        groups = [(at, min(at + 4, lines)) for at in range(0, lines, 4)]
    sums = None
    for at, end in groups:
        sums = apply_pairs(own, beside, partners[at:end], weights, at, side, sums)
    mine, far = sums
    near = swap(far)
    away = lax.ppermute(jnp.where(core == column, near, mine), "kb", across)
    applied, gram = join(mine, near, away, orbitals.shape)
    if blocks_per_k > 1:
        gram = block_gram(orbitals, applied, owner, blocks_per_k, side**3)
    return applied, gram


def solution(mesh):
    in_specs = (P(None, ("grp", "kb"), "slab", None), P(None, None, "slab"), P(), P())
    out_specs = (P(None, ("grp", "kb"), "slab", None), P(None, ("grp", "kb"), None))
    return jax.shard_map(
        on_device, mesh=mesh, in_specs=in_specs, out_specs=out_specs, check_vma=False
    )
```

```python
import functools
import math

import jax
import jax.numpy as jnp
import numpy as np
from jax import lax
from jax.experimental import pallas as pl
from jax.experimental.pallas import tpu as pltpu
from jax.sharding import PartitionSpec as P

NK = 8
SUBLANES = 8
STEP = 9
GROUP = 4
LANES = 128
F32 = jnp.float32
BF16 = jnp.bfloat16


def bf16_parts(table):
    high = table.astype(np.float32).astype(BF16)
    low = (table - high.astype(np.float64)).astype(np.float32).astype(BF16)
    return np.stack([high, low])


def lane_table(side):
    lows = LANES // side
    index = np.arange(LANES)
    low, z = index // side, index % side
    phase = 2.0 * math.pi * (np.outer(low, low) / lows + np.outer(z, z) / side)
    real, imag = np.cos(phase), -np.sin(phase)
    return np.block([[real, imag], [-imag, real]])


def turn_table(side):
    phase = 2.0 * math.pi * np.arange(side // 2) / side
    both = np.stack([np.cos(phase), np.sin(phase)]).astype(np.float32)
    return np.ascontiguousarray(np.broadcast_to(both[..., None], (*both.shape, LANES)))


def twist_table(side, rows):
    tiles = side * side // LANES
    phase = 2.0 * math.pi * np.outer(np.arange(tiles), np.arange(LANES) // side) / side
    both = np.stack([np.cos(phase), np.sin(phase)], 1).astype(np.float32)
    return np.ascontiguousarray(np.broadcast_to(both[:, :, None], (tiles, 2, rows, LANES)))


def split(value):
    high = value.astype(BF16)
    return high, (value - high.astype(F32)).astype(BF16)


def dot_parts(left, right):
    dot = functools.partial(jnp.dot, preferred_element_type=F32)
    return dot(left[0], right[0]) + (dot(left[1], right[0]) + dot(left[0], right[1]))


def dft_list(values, sign):
    count = len(values)
    if count == 1:
        return values
    even, odd = dft_list(values[0::2], sign), dft_list(values[1::2], sign)
    first, second = [], []
    for k in range(count // 2):
        re, im = odd[k]
        eighth = 8 * k // count if 8 * k % count == 0 else None
        if eighth == 0:
            pass
        elif eighth == 2:
            re, im = (-im, re) if sign > 0 else (im, -re)
        elif eighth == 1:
            root = math.sqrt(0.5)
            re, im = (
                ((re - im) * root, (re + im) * root)
                if sign > 0
                else ((re + im) * root, (im - re) * root)
            )
        elif eighth == 3:
            root = math.sqrt(0.5)
            re, im = (
                ((-re - im) * root, (re - im) * root)
                if sign > 0
                else ((im - re) * root, (-re - im) * root)
            )
        else:
            angle = 2.0 * math.pi * k / count
            cosine, sine = math.cos(angle), sign * math.sin(angle)
            re, im = re * cosine - im * sine, re * sine + im * cosine
        first.append((even[k][0] + re, even[k][1] + im))
        second.append((even[k][0] - re, even[k][1] - im))
    return first + second


def lane_slice(tile):
    return pl.ds(tile * LANES, LANES)


def weight_kernel(side, blocks_per_k, order, late, q_ref, owner_ref, mine_ref, other_ref, weight_ref):
    tiles = side * side // LANES
    lows = LANES // side
    scale = -1.0 / (NK * side**3)
    place, core = lax.axis_index("kb"), lax.axis_index("slab")
    line, column = place // 2, place % 2
    first_core = core == 0
    lane = lax.broadcasted_iota(jnp.int32, (side, LANES), 1) // side
    pairs = [(2 * line + core, 2 * (line ^ d) + column) for d in order]
    if late is not None:
        pairs.append((place, 2 * (line ^ late) + (column ^ core)))
    for pair, (target_at, partner_at) in enumerate(pairs):
        q = q_ref[owner_ref[target_at] // blocks_per_k, owner_ref[partner_at] // blocks_per_k]
        mine, other = mine_ref[q], other_ref[q]
        low_half = jnp.where(first_core, mine, other) * scale
        high_half = jnp.where(first_core, other, mine) * scale
        for b in range(tiles):
            total = None
            for a in range(lows):
                row = a * tiles + b
                source, chunk = row // lows, row % lows
                half = low_half if source < tiles // 2 else high_half
                at = source % (tiles // 2) * LANES
                piece = half[:, at : at + LANES]
                shift = (a - chunk) % lows * side
                if shift:
                    piece = pltpu.roll(piece, shift, 1)
                total = piece if total is None else jnp.where(lane == a, piece, total)
            at = pl.ds(b // GROUP * GROUP * side + b % GROUP, side, stride=GROUP)
            weight_ref[pair, at, :] = total


def pair_kernel(side, count, first, late, has_sum, *refs):
    refs = list(refs)
    take = lambda n: [refs.pop(0) for _ in range(n)]
    partners = [take(1 if late else 2) for _ in range(count)]
    own = take(2)
    beside = None if late else take(2)
    (weight_ref,) = take(1)
    lane_f, lane_b, twist, turn = take(4)
    sums = take(2) if has_sum else None
    outs = take(3 if late else 2)
    target, x_re, x_im, high_ref, low_ref, g_ref = take(6)

    tiles = side * side // LANES
    half = side // 2
    subs = 2 * GROUP
    rows = half * subs

    def parts(ref):
        return ref[0], ref[1]

    if late:
        for h in range(2):
            target[h] = own[h][:, 0]
        partners = [[whole.at[0:2], whole.at[2:4]] for (whole,) in partners]
    else:
        home = lax.axis_index("kb") % 2 == lax.axis_index("slab")
        for h in range(2):
            target[h] = jnp.where(home, own[h][:, 0], beside[h][:, 0])

    groups = tiles // GROUP

    def spread(p, b, x, parity):
        start = ((p * groups + b // GROUP) * half + x) * STEP + parity * GROUP + b % GROUP
        return pl.ds(start, SUBLANES, stride=STEP)

    def packed(g, x):
        return pl.ds((g * half + x) * STEP, subs)

    def densities(p):
        for x in range(0, half, SUBLANES):
            block = pl.ds(x, SUBLANES)
            both = []
            for h in range(2):
                values = []
                for t in range(tiles):
                    t_re, t_im = target[h, 0, block, lane_slice(t)], target[h, 1, block, lane_slice(t)]
                    p_re = partners[p][h][0, 0, block, lane_slice(t)]
                    p_im = partners[p][h][1, 0, block, lane_slice(t)]
                    values.append((p_re * t_re + p_im * t_im, p_re * t_im - p_im * t_re))
                both.append(dft_list(values, -1))
            turn_re, turn_im = turn[0, block], turn[1, block]
            for b in range(tiles):
                (re_0, im_0), (re_1, im_1) = both[0][b], both[1][b]
                re, im = re_0 - re_1, im_0 - im_1
                even = re_0 + re_1, im_0 + im_1
                odd = re * turn_re + im * turn_im, im * turn_re - re * turn_im
                for parity, (re, im) in enumerate((even, odd)):
                    if b:
                        cosine, sine = twist[b, 0], twist[b, 1]
                        re, im = re * cosine + im * sine, im * cosine - re * sine
                    x_re[spread(p, b, x, parity), :] = re
                    x_im[spread(p, b, x, parity), :] = im

    def forward(g):
        values = [(x_re[packed(g, x), :], x_im[packed(g, x), :]) for x in range(half)]
        values = dft_list(values, -1)
        for x in range(0, half, 2):
            at = pl.ds(g * rows + x * subs, 2 * subs)
            for k in range(2):
                high, low = split(jnp.concatenate([values[x][k], values[x + 1][k]], 0))
                high_ref[at, lane_slice(k)] = high
                low_ref[at, lane_slice(k)] = low

    def middle(g):
        at = pl.ds(g * rows, rows)
        spectrum = dot_parts((high_ref[at, :], low_ref[at, :]), parts(lane_f))
        weights = weight_ref[first + g // groups, pl.ds(g % groups * rows, rows), :]
        weighted = split(spectrum * jnp.concatenate([weights, weights], 1))
        g_ref[at, :] = dot_parts(weighted, parts(lane_b))

    def backward(g):
        values = []
        for x in range(half):
            at = pl.ds(g * rows + x * subs, subs)
            values.append((g_ref[at, lane_slice(0)], g_ref[at, lane_slice(1)]))
        for x, (re, im) in enumerate(dft_list(values, 1)):
            x_re[packed(g, x), :] = re
            x_im[packed(g, x), :] = im

    for p in range(count):
        densities(p)
        for g in range(p * groups, (p + 1) * groups):
            forward(g)
            middle(g)
            backward(g)
    gram_re = jnp.zeros((SUBLANES, LANES), F32)
    gram_im = jnp.zeros((SUBLANES, LANES), F32)
    for x in range(0, half, SUBLANES):
        block = pl.ds(x, SUBLANES)
        total = [[[0.0, 0.0] for _ in range(tiles)] for _ in range(2)]
        if has_sum:
            for h in range(2):
                for t in range(tiles):
                    for k in range(2):
                        total[h][t][k] = sums[h][pl.ds((k * tiles + t) * half + x, SUBLANES), :]
        turn_re, turn_im = turn[0, block], turn[1, block]
        for p in range(count):
            both = [], []
            for b in range(tiles):
                pair = []
                for parity in range(2):
                    re, im = x_re[spread(p, b, x, parity), :], x_im[spread(p, b, x, parity), :]
                    if b:
                        cosine, sine = twist[b, 0], twist[b, 1]
                        re, im = re * cosine - im * sine, im * cosine + re * sine
                    pair.append((re, im))
                re, im = pair[1]
                re, im = re * turn_re - im * turn_im, im * turn_re + re * turn_im
                both[0].append((pair[0][0] + re, pair[0][1] + im))
                both[1].append((pair[0][0] - re, pair[0][1] - im))
            for h in range(2):
                for t, (re, im) in enumerate(dft_list(both[h], 1)):
                    p_re = partners[p][h][0, 0, block, lane_slice(t)]
                    p_im = partners[p][h][1, 0, block, lane_slice(t)]
                    total[h][t][0] = total[h][t][0] + (p_re * re - p_im * im)
                    total[h][t][1] = total[h][t][1] + (p_re * im + p_im * re)
        for h in range(2):
            for t in range(tiles):
                re, im = total[h][t]
                t_re, t_im = target[h, 0, block, lane_slice(t)], target[h, 1, block, lane_slice(t)]
                gram_re += t_re * re + t_im * im
                gram_im += t_re * im - t_im * re
                outs[h][pl.ds(t * half + x, SUBLANES), :] = re
                if late and h:
                    outs[2][pl.ds(t * half + x, SUBLANES), :] = im
                else:
                    outs[h][pl.ds((tiles + t) * half + x, SUBLANES), :] = im
    end = 2 * tiles * half
    scale = 1.0 / side**3
    sums_row = jnp.concatenate(
        [
            jnp.full((4, LANES), jnp.sum(gram_re) * scale, F32),
            jnp.full((4, LANES), jnp.sum(gram_im) * scale, F32),
        ],
        0,
    )
    outs[0][pl.ds(end, 8), :] = sums_row
    outs[1][pl.ds(end // 2 if late else end, 8), :] = sums_row


def join_kernel(*refs):
    *parts, applied_ref, gram_ref = refs
    own, near, away_mine, away_near, *late = parts
    half = applied_ref.shape[2]
    tiles = applied_ref.shape[3] // LANES
    home = lax.axis_index("kb") % 2 == lax.axis_index("slab")

    def total(k, at, size):
        at_all = pl.ds(at if k == 0 else tiles * half + at, size)
        found = jnp.where(home, own[at_all, :], near[at_all, :]) + jnp.where(
            home, away_mine[at_all, :], away_near[at_all, :]
        )
        if late:
            found += late[0][at_all, :] + late[1 + k][pl.ds(at, size), :]
        return found

    for k in range(2):
        for t in range(tiles):
            applied_ref[k, 0, :, lane_slice(t)] = total(k, t * half, half)
    end = pl.ds(2 * tiles * half, 8)
    sums = jnp.where(home, own[end, :], near[end, :]) + jnp.where(
        home, away_mine[end, :], away_near[end, :]
    )
    if late:
        sums += late[0][end, :] + late[1][pl.ds(tiles * half, 8), :]
    gram_ref[0, 0, 0] = jnp.max(sums[0:1, :])
    gram_ref[0, 0, 1] = jnp.max(sums[4:5, :])


VMEM = pl.BlockSpec(memory_space=pltpu.VMEM)
SMEM = pl.BlockSpec(memory_space=pltpu.SMEM)


COST = pl.CostEstimate(flops=1, bytes_accessed=1, transcendentals=0)


def params():
    return pltpu.CompilerParams(vmem_limit_bytes=48 * 2**20)


def choose_weights(q_index, owner, kernels, order, late, side, blocks_per_k):
    count = len(order) + (late is not None)
    return pl.pallas_call(
        functools.partial(weight_kernel, side, blocks_per_k, order, late),
        out_shape=jax.ShapeDtypeStruct((count, side**3 // LANES, LANES), F32),
        in_specs=[SMEM, SMEM, VMEM, VMEM],
        out_specs=VMEM,
        compiler_params=params(),
        cost_estimate=COST,
        name="weights",
    )(q_index, owner, *kernels)


def apply_pairs(own, beside, partners, weights, first, side, sums=None, late=False):
    count = len(partners)
    half = side // 2
    tiles = side * side // LANES
    rows = count * side**3 // LANES
    lane = lane_table(side)
    tables = [
        jnp.asarray(bf16_parts(lane)),
        jnp.asarray(bf16_parts(lane.T)),
        jnp.asarray(twist_table(side, SUBLANES)),
        jnp.asarray(turn_table(side)),
    ]
    operands = [x for pair in partners for x in pair] + [*own, *beside, weights, *tables]
    operands += list(sums) if sums is not None else []
    shapes = [2 * tiles * half + 8] * 2
    if late:
        shapes[1:] = [tiles * half + 8, tiles * half]
    messages = tuple(jax.ShapeDtypeStruct((n, LANES), F32) for n in shapes)
    return pl.pallas_call(
        functools.partial(pair_kernel, side, count, first, late, sums is not None),
        out_shape=messages,
        in_specs=[VMEM] * len(operands),
        out_specs=(VMEM,) * len(messages),
        scratch_shapes=[
            pltpu.VMEM((2, 2, half, side * side), F32),
            pltpu.VMEM((rows // SUBLANES * STEP, LANES), F32),
            pltpu.VMEM((rows // SUBLANES * STEP, LANES), F32),
            pltpu.VMEM((rows, 2 * LANES), BF16),
            pltpu.VMEM((rows, 2 * LANES), BF16),
            pltpu.VMEM((rows, 2 * LANES), F32),
        ],
        compiler_params=params(),
        cost_estimate=COST,
        name="pairs",
    )(*operands)


def join(parts, shape):
    applied, gram = pl.pallas_call(
        join_kernel,
        out_shape=(jax.ShapeDtypeStruct(shape, F32), jax.ShapeDtypeStruct((1, 1, 2), F32)),
        in_specs=[VMEM] * len(parts),
        out_specs=(VMEM, SMEM),
        compiler_params=params(),
        cost_estimate=COST,
        name="join",
    )(*parts)
    return applied, gram.transpose(2, 0, 1)


def block_gram(orbitals, applied, owner, blocks_per_k, cells):
    highest = lax.Precision.HIGHEST
    partners = lax.all_gather(orbitals, "kb", axis=1, tiled=True)
    re = jnp.einsum("pxa,txa->tp", partners[0], applied[0], precision=highest)
    re += jnp.einsum("pxa,txa->tp", partners[1], applied[1], precision=highest)
    im = jnp.einsum("pxa,txa->tp", partners[0], applied[1], precision=highest)
    im -= jnp.einsum("pxa,txa->tp", partners[1], applied[0], precision=highest)
    sums = lax.psum(jnp.stack([re, im]) / cells, "slab")
    own = owner[lax.axis_index("kb")] // blocks_per_k
    wanted = own * blocks_per_k + jnp.arange(blocks_per_k, dtype=jnp.int32)
    selector = jnp.where(owner[:, None] == wanted[None], 1.0, 0.0).astype(F32)
    return jnp.einsum("ktp,pc->ktc", sums, selector, precision=highest)


def on_device(orbitals, kernel, q_index, owner):
    side = kernel.shape[1]
    n_kb = lax.axis_size("kb")
    lines = n_kb // 2
    blocks_per_k = n_kb // NK
    place, core = lax.axis_index("kb"), lax.axis_index("slab")
    column = place % 2
    across = [(a, a ^ 1) for a in range(n_kb)]

    def swap(x):
        return lax.ppermute(x, "slab", [(0, 1), (1, 0)])

    def from_line(x, d):
        return lax.ppermute(
            x, "kb", [(2 * a + c, 2 * (a ^ d) + c) for a in range(lines) for c in range(2)]
        )

    late = 3 if lines == 4 else None
    order = [d for d in range(lines) if d != late]
    first = [*order[2:], 1, 0]
    own = (orbitals, swap(orbitals))
    arrived = {d: from_line(orbitals, d) for d in order[1:]}
    arrived[0] = lax.ppermute(orbitals, "kb", across)
    weights = choose_weights(
        q_index, owner, (kernel, swap(kernel)), tuple(order), late, side, blocks_per_k
    )
    landed = lax.optimization_barrier((*(arrived[d] for d in first), weights))
    arrived.update(zip(first, landed))
    weights = landed[-1]
    far = {d: swap(arrived[d]) for d in first}
    beside = (arrived[0], far[0])
    partners = [own] + [(arrived[d], far[d]) for d in order[1:]]
    sums = None
    for at in range(0, len(order), 4):
        sums = apply_pairs(own, beside, partners[at : at + 4], weights, at, side, sums)
    if late is not None:
        steps = (2 * late, 2 * late + 1)
        moves = [(2 * a + c, 2 * (a ^ steps[c]) + c) for a in range(n_kb) for c in range(2)]
        last = lax.ppermute(jnp.concatenate(own), ("kb", "slab"), moves)
        last, _ = lax.optimization_barrier((last, sums))
    mine, other_rows = sums
    crossed = [
        (2 * a + core, 2 * (a ^ 1) + 1 - core) for a in range(n_kb) for core in range(2)
    ]
    parts = [
        mine,
        swap(other_rows),
        lax.ppermute(mine, "kb", across),
        lax.ppermute(other_rows, ("kb", "slab"), crossed),
    ]
    if late is not None:
        late_mine, *late_rows = apply_pairs(
            own, (), [(last,)], weights, len(order), side, late=True
        )
        parts += [late_mine, *(swap(x) for x in late_rows)]
    applied, gram = join(parts, orbitals.shape)
    if blocks_per_k > 1:
        gram = block_gram(orbitals, applied, owner, blocks_per_k, side**3)
    return applied, gram


def solution(mesh):
    in_specs = (P(None, ("grp", "kb"), "slab", None), P(None, None, "slab"), P(), P())
    out_specs = (P(None, ("grp", "kb"), "slab", None), P(None, ("grp", "kb"), None))
    return jax.shard_map(
        on_device, mesh=mesh, in_specs=in_specs, out_specs=out_specs, check_vma=False
    )
```

```python
import functools
import math

import jax
import jax.numpy as jnp
import numpy as np
from jax import lax
from jax.experimental import pallas as pl
from jax.experimental.pallas import tpu as pltpu
from jax.sharding import PartitionSpec as P

NK = 8
SUBLANES = 8
STEP = 9
GROUP = 4
LANES = 128
F32 = jnp.float32
BF16 = jnp.bfloat16


def bf16_parts(table):
    high = table.astype(np.float32).astype(BF16)
    low = (table - high.astype(np.float64)).astype(np.float32).astype(BF16)
    return np.stack([high, low])


def lane_table(side):
    lows = LANES // side
    index = np.arange(LANES)
    low, z = index // side, index % side
    phase = 2.0 * math.pi * (np.outer(low, low) / lows + np.outer(z, z) / side)
    real, imag = np.cos(phase), -np.sin(phase)
    return np.block([[real, imag], [-imag, real]])


def turn_table(side):
    phase = 2.0 * math.pi * np.arange(side // 2) / side
    both = np.stack([np.cos(phase), np.sin(phase)]).astype(np.float32)
    return np.ascontiguousarray(np.broadcast_to(both[..., None], (*both.shape, LANES)))


def twist_table(side, rows):
    tiles = side * side // LANES
    phase = 2.0 * math.pi * np.outer(np.arange(tiles), np.arange(LANES) // side) / side
    both = np.stack([np.cos(phase), np.sin(phase)], 1).astype(np.float32)
    return np.ascontiguousarray(np.broadcast_to(both[:, :, None], (tiles, 2, rows, LANES)))


def split(value):
    high = value.astype(BF16)
    return high, (value - high.astype(F32)).astype(BF16)


def dot_parts(left, right):
    dot = functools.partial(jnp.dot, preferred_element_type=F32)
    return dot(left[0], right[0]) + (dot(left[1], right[0]) + dot(left[0], right[1]))


def dft_list(values, sign):
    count = len(values)
    if count == 1:
        return values
    even, odd = dft_list(values[0::2], sign), dft_list(values[1::2], sign)
    first, second = [], []
    for k in range(count // 2):
        re, im = odd[k]
        eighth = 8 * k // count if 8 * k % count == 0 else None
        if eighth == 0:
            pass
        elif eighth == 2:
            re, im = (-im, re) if sign > 0 else (im, -re)
        elif eighth == 1:
            root = math.sqrt(0.5)
            re, im = (
                ((re - im) * root, (re + im) * root)
                if sign > 0
                else ((re + im) * root, (im - re) * root)
            )
        elif eighth == 3:
            root = math.sqrt(0.5)
            re, im = (
                ((-re - im) * root, (re - im) * root)
                if sign > 0
                else ((im - re) * root, (-re - im) * root)
            )
        else:
            angle = 2.0 * math.pi * k / count
            cosine, sine = math.cos(angle), sign * math.sin(angle)
            re, im = re * cosine - im * sine, re * sine + im * cosine
        first.append((even[k][0] + re, even[k][1] + im))
        second.append((even[k][0] - re, even[k][1] - im))
    return first + second


def lane_slice(tile):
    return pl.ds(tile * LANES, LANES)


def weight_kernel(side, blocks_per_k, order, late, q_ref, owner_ref, mine_ref, other_ref, weight_ref):
    tiles = side * side // LANES
    lows = LANES // side
    scale = -1.0 / (NK * side**3)
    place, core = lax.axis_index("kb"), lax.axis_index("slab")
    line, column = place // 2, place % 2
    first_core = core == 0
    lane = lax.broadcasted_iota(jnp.int32, (side, LANES), 1) // side
    targets = (place, place ^ 1)
    pairs = [(target, 2 * (line ^ d) + column) for target in targets for d in order]
    if late is not None:
        pairs.append((place, 2 * (line ^ late) + (column ^ core)))
    for pair, (target_at, partner_at) in enumerate(pairs):
        q = q_ref[owner_ref[target_at] // blocks_per_k, owner_ref[partner_at] // blocks_per_k]
        mine, other = mine_ref[q], other_ref[q]
        low_half = jnp.where(first_core, mine, other) * scale
        high_half = jnp.where(first_core, other, mine) * scale
        for b in range(tiles):
            total = None
            for a in range(lows):
                row = a * tiles + b
                source, chunk = row // lows, row % lows
                half = low_half if source < tiles // 2 else high_half
                at = source % (tiles // 2) * LANES
                piece = half[:, at : at + LANES]
                shift = (a - chunk) % lows * side
                if shift:
                    piece = pltpu.roll(piece, shift, 1)
                total = piece if total is None else jnp.where(lane == a, piece, total)
            at = pl.ds(b // GROUP * GROUP * side + b % GROUP, side, stride=GROUP)
            weight_ref[pair, at, :] = total


def pair_kernel(side, count, at_weights, late, has_sum, *refs):
    refs = list(refs)
    take = lambda n: [refs.pop(0) for _ in range(n)]
    partners = [take(1 if late else 2) for _ in range(count)]
    targets = [take(2) for _ in range(1 if late else 2)]
    (weight_ref,) = take(1)
    lane_f, lane_b, twist, turn = take(4)
    sums = take(2) if has_sum else None
    before = take(2) if late else None
    outs = take(3)
    x_re, x_im, high_ref, low_ref, f_ref, back_high, back_low, g_ref = take(8)
    if late:
        partners = [[whole.at[0:2], whole.at[2:4]] for (whole,) in partners]

    tiles = side * side // LANES
    half = side // 2
    subs = 2 * GROUP
    rows = half * subs
    groups = tiles // GROUP
    halves = 2 if late else 1

    def parts(ref):
        return ref[0], ref[1]

    def field(band, h, block, t):
        return band[h][0, 0, block, lane_slice(t)], band[h][1, 0, block, lane_slice(t)]

    def spread(pair, b, x, parity):
        start = ((pair * groups + b // GROUP) * half + x) * STEP + parity * GROUP + b % GROUP
        return pl.ds(start, SUBLANES, stride=STEP)

    def packed(g, x):
        return pl.ds((g * half + x) * STEP, subs)

    def densities(pair, target, partner):
        for x in range(0, half, SUBLANES):
            block = pl.ds(x, SUBLANES)
            both = []
            for h in range(2):
                values = []
                for t in range(tiles):
                    t_re, t_im = field(target, h, block, t)
                    p_re, p_im = field(partner, h, block, t)
                    values.append((p_re * t_re + p_im * t_im, p_re * t_im - p_im * t_re))
                both.append(dft_list(values, -1))
            turn_re, turn_im = turn[0, block], turn[1, block]
            for b in range(tiles):
                (re_0, im_0), (re_1, im_1) = both[0][b], both[1][b]
                re, im = re_0 - re_1, im_0 - im_1
                even = re_0 + re_1, im_0 + im_1
                odd = re * turn_re + im * turn_im, im * turn_re - re * turn_im
                for parity, (re, im) in enumerate((even, odd)):
                    if b:
                        cosine, sine = twist[b, 0], twist[b, 1]
                        re, im = re * cosine + im * sine, im * cosine - re * sine
                    x_re[spread(pair, b, x, parity), :] = re
                    x_im[spread(pair, b, x, parity), :] = im

    def transform(g, weights):
        values = [(x_re[packed(g, x), :], x_im[packed(g, x), :]) for x in range(half)]
        values = dft_list(values, -1)
        for x in range(0, half, 2):
            at = pl.ds(g * rows + x * subs, 2 * subs)
            for k in range(2):
                high, low = split(jnp.concatenate([values[x][k], values[x + 1][k]], 0))
                high_ref[at, lane_slice(k)] = high
                low_ref[at, lane_slice(k)] = low
        at = pl.ds(g * rows, rows)
        spectrum = dot_parts((high_ref[at, :], low_ref[at, :]), parts(lane_f))
        f_ref[at, :] = spectrum * jnp.concatenate([weights, weights], 1)
        values = []
        for x in range(half):
            at = pl.ds(g * rows + x * subs, subs)
            values.append((f_ref[at, lane_slice(0)], f_ref[at, lane_slice(1)]))
        for x, (re, im) in enumerate(dft_list(values, 1)):
            x_re[packed(g, x), :] = re
            x_im[packed(g, x), :] = im

    def potentials(pair):
        for b in range(tiles):
            made = [[] for _ in range(halves)]
            for x in range(0, half, SUBLANES):
                block = pl.ds(x, SUBLANES)
                turn_re, turn_im = turn[0, block], turn[1, block]
                even_re, even_im = x_re[spread(pair, b, x, 0), :], x_im[spread(pair, b, x, 0), :]
                re, im = x_re[spread(pair, b, x, 1), :], x_im[spread(pair, b, x, 1), :]
                re, im = re * turn_re - im * turn_im, im * turn_re + re * turn_im
                made[0].append((even_re + re, even_im + im))
                if late:
                    made[1].append((even_re - re, even_im - im))
            for h in range(halves):
                at = pl.ds(((pair * halves + h) * tiles + b) * half, half)
                for k in range(2):
                    high, low = split(jnp.concatenate([block[k] for block in made[h]], 0))
                    back_high[at, lane_slice(k)] = high
                    back_low[at, lane_slice(k)] = low
        at = pl.ds(pair * halves * tiles * half, halves * tiles * half)
        g_ref[at, :] = dot_parts((back_high[at, :], back_low[at, :]), parts(lane_b))

    for c, target in enumerate(targets):
        for p, partner in enumerate(partners):
            pair = c * count + p
            densities(pair, target, partner)
            for g in range(groups):
                weights = weight_ref[at_weights[c] + p, pl.ds(g * rows, rows), :]
                transform(pair * groups + g, weights)
            potentials(pair)
    for c, target in enumerate(targets):
        gram_re = jnp.zeros((SUBLANES, LANES), F32)
        gram_im = jnp.zeros((SUBLANES, LANES), F32)
        for h in range(halves):
            for x in range(0, half, SUBLANES):
                block = pl.ds(x, SUBLANES)
                total = [[0.0, 0.0] for _ in range(tiles)]
                if has_sum:
                    for t in range(tiles):
                        for k in range(2):
                            total[t][k] = sums[c][pl.ds((k * tiles + t) * half + x, SUBLANES), :]
                for p, partner in enumerate(partners):
                    values = []
                    for b in range(tiles):
                        pair = c * count + p
                        start = ((pair * halves + h) * tiles + b) * half + x
                        at = pl.ds(start, SUBLANES)
                        re, im = g_ref[at, lane_slice(0)], g_ref[at, lane_slice(1)]
                        if b:
                            cosine, sine = twist[b, 0], twist[b, 1]
                            re, im = re * cosine - im * sine, im * cosine + re * sine
                        values.append((re, im))
                    for t, (re, im) in enumerate(dft_list(values, 1)):
                        p_re, p_im = field(partner, h, block, t)
                        total[t][0] = total[t][0] + (p_re * re - p_im * im)
                        total[t][1] = total[t][1] + (p_re * im + p_im * re)
                for t in range(tiles):
                    re, im = total[t]
                    t_re, t_im = field(target, h, block, t)
                    gram_re += t_re * re + t_im * im
                    gram_im += t_re * im - t_im * re
                    if late and h:
                        outs[1][pl.ds(t * half + x, SUBLANES), :] = re
                        outs[2][pl.ds(t * half + x, SUBLANES), :] = im
                    else:
                        outs[c][pl.ds(t * half + x, SUBLANES), :] = re
                        outs[c][pl.ds((tiles + t) * half + x, SUBLANES), :] = im
        end = 2 * tiles * half
        scale = 1.0 / side**3
        sums_row = jnp.concatenate(
            [
                jnp.full((4, LANES), jnp.sum(gram_re) * scale, F32),
                jnp.full((4, LANES), jnp.sum(gram_im) * scale, F32),
            ],
            0,
        )
        if late:
            sums_row += before[0][pl.ds(end, 8), :] + before[1][...]
            outs[0][pl.ds(end, 8), :] = sums_row
            outs[1][pl.ds(end // 2, 8), :] = sums_row
        else:
            outs[c][pl.ds(end, 8), :] = sums_row
            if c:
                outs[2][...] = sums_row


def join_kernel(*refs):
    home, away, *late, applied_ref, gram_ref = refs
    half = applied_ref.shape[2]
    tiles = applied_ref.shape[3] // LANES
    for k in range(2):
        for t in range(tiles):
            at = pl.ds((k * tiles + t) * half, half)
            found = home[at, :] + away[at, :]
            if late:
                found += late[0][at, :] + late[1 + k][pl.ds(t * half, half), :]
            applied_ref[k, 0, :, lane_slice(t)] = found
    if late:
        gram = late[0][pl.ds(2 * tiles * half, 8), :] + late[1][pl.ds(tiles * half, 8), :]
    else:
        gram = home[pl.ds(2 * tiles * half, 8), :]
    gram_ref[0, 0, 0] = jnp.max(gram[0:1, :])
    gram_ref[0, 0, 1] = jnp.max(gram[4:5, :])


VMEM = pl.BlockSpec(memory_space=pltpu.VMEM)
SMEM = pl.BlockSpec(memory_space=pltpu.SMEM)


COST = pl.CostEstimate(flops=1, bytes_accessed=1, transcendentals=0)

LATE_COST = pl.CostEstimate(flops=2 * 10**9, bytes_accessed=4 * 2**20, transcendentals=0)


def params():
    return pltpu.CompilerParams(vmem_limit_bytes=48 * 2**20)


def choose_weights(q_index, owner, kernels, order, late, side, blocks_per_k):
    count = 2 * len(order) + (late is not None)
    return pl.pallas_call(
        functools.partial(weight_kernel, side, blocks_per_k, order, late),
        out_shape=jax.ShapeDtypeStruct((count, side**3 // LANES, LANES), F32),
        in_specs=[SMEM, SMEM, VMEM, VMEM],
        out_specs=VMEM,
        compiler_params=params(),
        cost_estimate=COST,
        name="weights",
    )(q_index, owner, *kernels)


def apply_pairs(targets, partners, weights, at_weights, side, sums=(), before=()):
    count, late = len(partners), len(targets) == 1
    half = side // 2
    tiles = side * side // LANES
    pairs = count * len(targets)
    rows = pairs * side**3 // LANES
    back = rows if late else rows // 2
    lane = lane_table(side)
    tables = [
        jnp.asarray(bf16_parts(lane)),
        jnp.asarray(bf16_parts(lane.T)),
        jnp.asarray(twist_table(side, SUBLANES)),
        jnp.asarray(turn_table(side)),
    ]
    operands = [x for pair in partners for x in pair] + [x for pair in targets for x in pair]
    operands += [weights, *tables, *sums, *before]
    size = 2 * tiles * half + 8
    sizes = [size, tiles * half + 8, tiles * half] if late else [size, size, 8]
    messages = tuple(jax.ShapeDtypeStruct((n, LANES), F32) for n in sizes)
    return pl.pallas_call(
        functools.partial(pair_kernel, side, count, at_weights, late, len(sums) > 0),
        out_shape=messages,
        in_specs=[VMEM] * len(operands),
        out_specs=(VMEM,) * len(messages),
        scratch_shapes=[
            pltpu.VMEM((rows // SUBLANES * STEP, LANES), F32),
            pltpu.VMEM((rows // SUBLANES * STEP, LANES), F32),
            pltpu.VMEM((rows, 2 * LANES), BF16),
            pltpu.VMEM((rows, 2 * LANES), BF16),
            pltpu.VMEM((rows, 2 * LANES), F32),
            pltpu.VMEM((back, 2 * LANES), BF16),
            pltpu.VMEM((back, 2 * LANES), BF16),
            pltpu.VMEM((back, 2 * LANES), F32),
        ],
        compiler_params=params(),
        cost_estimate=LATE_COST if late else COST,
        name="pairs",
    )(*operands)


def join(parts, shape):
    applied, gram = pl.pallas_call(
        join_kernel,
        out_shape=(jax.ShapeDtypeStruct(shape, F32), jax.ShapeDtypeStruct((1, 1, 2), F32)),
        in_specs=[VMEM] * len(parts),
        out_specs=(VMEM, SMEM),
        compiler_params=params(),
        cost_estimate=COST,
        name="join",
    )(*parts)
    return applied, gram.transpose(2, 0, 1)


def block_gram(orbitals, applied, owner, blocks_per_k, cells):
    highest = lax.Precision.HIGHEST
    partners = lax.all_gather(orbitals, "kb", axis=1, tiled=True)
    re = jnp.einsum("pxa,txa->tp", partners[0], applied[0], precision=highest)
    re += jnp.einsum("pxa,txa->tp", partners[1], applied[1], precision=highest)
    im = jnp.einsum("pxa,txa->tp", partners[0], applied[1], precision=highest)
    im -= jnp.einsum("pxa,txa->tp", partners[1], applied[0], precision=highest)
    sums = lax.psum(jnp.stack([re, im]) / cells, "slab")
    own = owner[lax.axis_index("kb")] // blocks_per_k
    wanted = own * blocks_per_k + jnp.arange(blocks_per_k, dtype=jnp.int32)
    selector = jnp.where(owner[:, None] == wanted[None], 1.0, 0.0).astype(F32)
    return jnp.einsum("ktp,pc->ktc", sums, selector, precision=highest)


def on_device(orbitals, kernel, q_index, owner):
    side = kernel.shape[1]
    n_kb = lax.axis_size("kb")
    lines = n_kb // 2
    blocks_per_k = n_kb // NK
    across = [(a, a ^ 1) for a in range(n_kb)]

    def swap(x):
        return lax.ppermute(x, "slab", [(0, 1), (1, 0)])

    def from_line(x, d):
        return lax.ppermute(
            x, "kb", [(2 * a + c, 2 * (a ^ d) + c) for a in range(lines) for c in range(2)]
        )

    late = 3 if lines == 4 else None
    order = [d for d in range(lines) if d != late]
    first = [*order[2:], 1, 0]
    own = (orbitals, swap(orbitals))
    arrived = {d: from_line(orbitals, d) for d in order[1:]}
    arrived[0] = lax.ppermute(orbitals, "kb", across)
    weights = choose_weights(
        q_index, owner, (kernel, swap(kernel)), tuple(order), late, side, blocks_per_k
    )
    landed = lax.optimization_barrier((*(arrived[d] for d in first), weights))
    arrived.update(zip(first, landed))
    weights = landed[-1]
    far = {d: swap(arrived[d]) for d in first}
    beside = (arrived[0], far[0])
    partners = [own] + [(arrived[d], far[d]) for d in order[1:]]
    sums = ()
    for at in range(0, len(order), 4):
        at_weights = (at, len(order) + at)
        sums = apply_pairs(
            (own, beside), partners[at : at + 4], weights, at_weights, side, sums[:2]
        )
    if late is not None:
        steps = (2 * late, 2 * late + 1)
        moves = [(2 * a + c, 2 * (a ^ steps[c]) + c) for a in range(n_kb) for c in range(2)]
        last = lax.ppermute(jnp.concatenate(own), ("kb", "slab"), moves)
        last, _ = lax.optimization_barrier((last, sums))
    home, away, away_sums = sums
    parts = [home, lax.ppermute(away, "kb", across)]
    if late is not None:
        crossed = [(2 * a + c, 2 * (a ^ 1) + 1 - c) for a in range(n_kb) for c in range(2)]
        crossed_sums = lax.ppermute(away_sums, ("kb", "slab"), crossed)
        late_mine, *late_rows = apply_pairs(
            (own,), [(last,)], weights, (2 * len(order),), side, before=(home, crossed_sums)
        )
        parts += [late_mine, *(swap(x) for x in late_rows)]
    applied, gram = join(parts, orbitals.shape)
    if blocks_per_k > 1:
        gram = block_gram(orbitals, applied, owner, blocks_per_k, side**3)
    return applied, gram


def solution(mesh):
    in_specs = (P(None, ("grp", "kb"), "slab", None), P(None, None, "slab"), P(), P())
    out_specs = (P(None, ("grp", "kb"), "slab", None), P(None, ("grp", "kb"), None))
    return jax.shard_map(
        on_device, mesh=mesh, in_specs=in_specs, out_specs=out_specs, check_vma=False
    )
```

```python
import functools
import math

import jax
import jax.numpy as jnp
import numpy as np
from jax import lax
from jax.experimental import pallas as pl
from jax.experimental.pallas import tpu as pltpu
from jax.sharding import PartitionSpec as P

NK = 8
SUBLANES = 8
STEP = 9
GROUP = 4
LANES = 128
F32 = jnp.float32
BF16 = jnp.bfloat16


def bf16_parts(table):
    high = table.astype(np.float32).astype(BF16)
    low = (table - high.astype(np.float64)).astype(np.float32).astype(BF16)
    return np.stack([high, low])


def lane_table(side):
    lows = LANES // side
    index = np.arange(LANES)
    low, z = index // side, index % side
    phase = 2.0 * math.pi * (np.outer(low, low) / lows + np.outer(z, z) / side)
    real, imag = np.cos(phase), -np.sin(phase)
    return np.block([[real, imag], [-imag, real]])


def turn_table(side):
    phase = 2.0 * math.pi * np.arange(side // 2) / side
    both = np.stack([np.cos(phase), np.sin(phase)]).astype(np.float32)
    return np.ascontiguousarray(np.broadcast_to(both[..., None], (*both.shape, LANES)))


def twist_table(side, rows):
    tiles = side * side // LANES
    phase = 2.0 * math.pi * np.outer(np.arange(tiles), np.arange(LANES) // side) / side
    both = np.stack([np.cos(phase), np.sin(phase)], 1).astype(np.float32)
    return np.ascontiguousarray(np.broadcast_to(both[:, :, None], (tiles, 2, rows, LANES)))


def split(value):
    high = value.astype(BF16)
    return high, (value - high.astype(F32)).astype(BF16)


def dot_parts(left, right):
    dot = functools.partial(jnp.dot, preferred_element_type=F32)
    return dot(left[0], right[0]) + (dot(left[1], right[0]) + dot(left[0], right[1]))


def dft_list(values, sign):
    count = len(values)
    if count == 1:
        return values
    even, odd = dft_list(values[0::2], sign), dft_list(values[1::2], sign)
    first, second = [], []
    for k in range(count // 2):
        re, im = odd[k]
        eighth = 8 * k // count if 8 * k % count == 0 else None
        if eighth == 0:
            pass
        elif eighth == 2:
            re, im = (-im, re) if sign > 0 else (im, -re)
        elif eighth == 1:
            root = math.sqrt(0.5)
            re, im = (
                ((re - im) * root, (re + im) * root)
                if sign > 0
                else ((re + im) * root, (im - re) * root)
            )
        elif eighth == 3:
            root = math.sqrt(0.5)
            re, im = (
                ((-re - im) * root, (re - im) * root)
                if sign > 0
                else ((im - re) * root, (-re - im) * root)
            )
        else:
            angle = 2.0 * math.pi * k / count
            cosine, sine = math.cos(angle), sign * math.sin(angle)
            re, im = re * cosine - im * sine, re * sine + im * cosine
        first.append((even[k][0] + re, even[k][1] + im))
        second.append((even[k][0] - re, even[k][1] - im))
    return first + second


def lane_slice(tile):
    return pl.ds(tile * LANES, LANES)


def weight_kernel(side, blocks_per_k, order, late, q_ref, owner_ref, mine_ref, other_ref, weight_ref):
    tiles = side * side // LANES
    lows = LANES // side
    scale = -1.0 / (NK * side**3)
    place, core = lax.axis_index("kb"), lax.axis_index("slab")
    line, column = place // 2, place % 2
    first_core = core == 0
    lane = lax.broadcasted_iota(jnp.int32, (side, LANES), 1) // side
    targets = (place, place ^ 1)
    pairs = [(target, 2 * (line ^ d) + column) for target in targets for d in order]
    if late is not None:
        pairs.append((place, 2 * (line ^ late) + (column ^ core)))
    for pair, (target_at, partner_at) in enumerate(pairs):
        q = q_ref[owner_ref[target_at] // blocks_per_k, owner_ref[partner_at] // blocks_per_k]
        mine, other = mine_ref[q], other_ref[q]
        low_half = jnp.where(first_core, mine, other) * scale
        high_half = jnp.where(first_core, other, mine) * scale
        for b in range(tiles):
            total = None
            for a in range(lows):
                row = a * tiles + b
                source, chunk = row // lows, row % lows
                half = low_half if source < tiles // 2 else high_half
                at = source % (tiles // 2) * LANES
                piece = half[:, at : at + LANES]
                shift = (a - chunk) % lows * side
                if shift:
                    piece = pltpu.roll(piece, shift, 1)
                total = piece if total is None else jnp.where(lane == a, piece, total)
            at = pl.ds(b // GROUP * GROUP * side + b % GROUP, side, stride=GROUP)
            weight_ref[pair, at, :] = total


def pair_kernel(side, count, at_weights, late, has_sum, *refs):
    refs = list(refs)
    take = lambda n: [refs.pop(0) for _ in range(n)]
    partners = [take(1 if late else 2) for _ in range(count)]
    targets = [take(2) for _ in range(1 if late else 2)]
    (weight_ref,) = take(1)
    lane_f, lane_b, twist, turn = take(4)
    sums = take(2) if has_sum else None
    before = take(2) if late else None
    outs = take(3)
    x_re, x_im, high_ref, low_ref, f_ref, back_high, back_low, g_ref = take(8)
    if late:
        partners = [[whole.at[0:2], whole.at[2:4]] for (whole,) in partners]

    tiles = side * side // LANES
    half = side // 2
    subs = 2 * GROUP
    rows = half * subs
    groups = tiles // GROUP
    halves = 2 if late else 1

    def parts(ref):
        return ref[0], ref[1]

    def field(band, h, block, t):
        return band[h][0, 0, block, lane_slice(t)], band[h][1, 0, block, lane_slice(t)]

    def spread(pair, b, x, parity):
        start = ((pair * groups + b // GROUP) * half + x) * STEP + parity * GROUP + b % GROUP
        return pl.ds(start, SUBLANES, stride=STEP)

    def packed(g, x):
        return pl.ds((g * half + x) * STEP, subs)

    def densities(pair, target, partner):
        for x in range(0, half, SUBLANES):
            block = pl.ds(x, SUBLANES)
            both = []
            for h in range(2):
                values = []
                for t in range(tiles):
                    t_re, t_im = field(target, h, block, t)
                    p_re, p_im = field(partner, h, block, t)
                    values.append((p_re * t_re + p_im * t_im, p_re * t_im - p_im * t_re))
                both.append(dft_list(values, -1))
            turn_re, turn_im = turn[0, block], turn[1, block]
            for b in range(tiles):
                (re_0, im_0), (re_1, im_1) = both[0][b], both[1][b]
                re, im = re_0 - re_1, im_0 - im_1
                even = re_0 + re_1, im_0 + im_1
                odd = re * turn_re + im * turn_im, im * turn_re - re * turn_im
                for parity, (re, im) in enumerate((even, odd)):
                    if b:
                        cosine, sine = twist[b, 0], twist[b, 1]
                        re, im = re * cosine + im * sine, im * cosine - re * sine
                    x_re[spread(pair, b, x, parity), :] = re
                    x_im[spread(pair, b, x, parity), :] = im

    def transform(g, weights):
        values = [(x_re[packed(g, x), :], x_im[packed(g, x), :]) for x in range(half)]
        values = dft_list(values, -1)
        for x in range(0, half, 2):
            at = pl.ds(g * rows + x * subs, 2 * subs)
            for k in range(2):
                high, low = split(jnp.concatenate([values[x][k], values[x + 1][k]], 0))
                high_ref[at, lane_slice(k)] = high
                low_ref[at, lane_slice(k)] = low
        at = pl.ds(g * rows, rows)
        spectrum = dot_parts((high_ref[at, :], low_ref[at, :]), parts(lane_f))
        f_ref[at, :] = spectrum * jnp.concatenate([weights, weights], 1)
        values = []
        for x in range(half):
            at = pl.ds(g * rows + x * subs, subs)
            values.append((f_ref[at, lane_slice(0)], f_ref[at, lane_slice(1)]))
        for x, (re, im) in enumerate(dft_list(values, 1)):
            x_re[packed(g, x), :] = re
            x_im[packed(g, x), :] = im

    def potentials(pair):
        for b in range(tiles):
            made = [[] for _ in range(halves)]
            for x in range(0, half, SUBLANES):
                block = pl.ds(x, SUBLANES)
                turn_re, turn_im = turn[0, block], turn[1, block]
                even_re, even_im = x_re[spread(pair, b, x, 0), :], x_im[spread(pair, b, x, 0), :]
                re, im = x_re[spread(pair, b, x, 1), :], x_im[spread(pair, b, x, 1), :]
                re, im = re * turn_re - im * turn_im, im * turn_re + re * turn_im
                made[0].append((even_re + re, even_im + im))
                if late:
                    made[1].append((even_re - re, even_im - im))
            for h in range(halves):
                at = pl.ds(((pair * halves + h) * tiles + b) * half, half)
                for k in range(2):
                    high, low = split(jnp.concatenate([block[k] for block in made[h]], 0))
                    back_high[at, lane_slice(k)] = high
                    back_low[at, lane_slice(k)] = low
        at = pl.ds(pair * halves * tiles * half, halves * tiles * half)
        g_ref[at, :] = dot_parts((back_high[at, :], back_low[at, :]), parts(lane_b))

    pairs = [(c, p) for c in range(len(targets)) for p in range(count)]
    for pair, (c, p) in enumerate(pairs):
        densities(pair, targets[c], partners[p])
    for pair, (c, p) in enumerate(pairs):
        for g in range(groups):
            weights = weight_ref[at_weights[c] + p, pl.ds(g * rows, rows), :]
            transform(pair * groups + g, weights)
    for pair in range(len(pairs)):
        potentials(pair)
    for c, target in enumerate(targets):
        gram_re = jnp.zeros((SUBLANES, LANES), F32)
        gram_im = jnp.zeros((SUBLANES, LANES), F32)
        for h in range(halves):
            for x in range(0, half, SUBLANES):
                block = pl.ds(x, SUBLANES)
                total = [[0.0, 0.0] for _ in range(tiles)]
                if has_sum:
                    for t in range(tiles):
                        for k in range(2):
                            total[t][k] = sums[c][pl.ds((k * tiles + t) * half + x, SUBLANES), :]
                for p, partner in enumerate(partners):
                    values = []
                    for b in range(tiles):
                        pair = c * count + p
                        start = ((pair * halves + h) * tiles + b) * half + x
                        at = pl.ds(start, SUBLANES)
                        re, im = g_ref[at, lane_slice(0)], g_ref[at, lane_slice(1)]
                        if b:
                            cosine, sine = twist[b, 0], twist[b, 1]
                            re, im = re * cosine - im * sine, im * cosine + re * sine
                        values.append((re, im))
                    for t, (re, im) in enumerate(dft_list(values, 1)):
                        p_re, p_im = field(partner, h, block, t)
                        total[t][0] = total[t][0] + (p_re * re - p_im * im)
                        total[t][1] = total[t][1] + (p_re * im + p_im * re)
                for t in range(tiles):
                    re, im = total[t]
                    t_re, t_im = field(target, h, block, t)
                    gram_re += t_re * re + t_im * im
                    gram_im += t_re * im - t_im * re
                    if late and h:
                        outs[1][pl.ds(t * half + x, SUBLANES), :] = re
                        outs[2][pl.ds(t * half + x, SUBLANES), :] = im
                    else:
                        outs[c][pl.ds(t * half + x, SUBLANES), :] = re
                        outs[c][pl.ds((tiles + t) * half + x, SUBLANES), :] = im
        end = 2 * tiles * half
        scale = 1.0 / side**3
        sums_row = jnp.concatenate(
            [
                jnp.full((4, LANES), jnp.sum(gram_re) * scale, F32),
                jnp.full((4, LANES), jnp.sum(gram_im) * scale, F32),
            ],
            0,
        )
        if late:
            sums_row += before[0][pl.ds(end, 8), :] + before[1][...]
            outs[0][pl.ds(end, 8), :] = sums_row
            outs[1][pl.ds(end // 2, 8), :] = sums_row
        else:
            outs[c][pl.ds(end, 8), :] = sums_row
            if c:
                outs[2][...] = sums_row


def join_kernel(*refs):
    home, away, *late, applied_ref, gram_ref = refs
    half = applied_ref.shape[2]
    tiles = applied_ref.shape[3] // LANES
    for k in range(2):
        for t in range(tiles):
            at = pl.ds((k * tiles + t) * half, half)
            found = home[at, :] + away[at, :]
            if late:
                found += late[0][at, :] + late[1 + k][pl.ds(t * half, half), :]
            applied_ref[k, 0, :, lane_slice(t)] = found
    if late:
        gram = late[0][pl.ds(2 * tiles * half, 8), :] + late[1][pl.ds(tiles * half, 8), :]
    else:
        gram = home[pl.ds(2 * tiles * half, 8), :]
    gram_ref[0, 0, 0] = jnp.max(gram[0:1, :])
    gram_ref[0, 0, 1] = jnp.max(gram[4:5, :])


VMEM = pl.BlockSpec(memory_space=pltpu.VMEM)
SMEM = pl.BlockSpec(memory_space=pltpu.SMEM)


COST = pl.CostEstimate(flops=1, bytes_accessed=1, transcendentals=0)

LATE_COST = pl.CostEstimate(flops=2 * 10**9, bytes_accessed=4 * 2**20, transcendentals=0)


def params():
    return pltpu.CompilerParams(vmem_limit_bytes=48 * 2**20)


def choose_weights(q_index, owner, kernels, order, late, side, blocks_per_k):
    count = 2 * len(order) + (late is not None)
    return pl.pallas_call(
        functools.partial(weight_kernel, side, blocks_per_k, order, late),
        out_shape=jax.ShapeDtypeStruct((count, side**3 // LANES, LANES), F32),
        in_specs=[SMEM, SMEM, VMEM, VMEM],
        out_specs=VMEM,
        compiler_params=params(),
        cost_estimate=COST,
        name="weights",
    )(q_index, owner, *kernels)


def apply_pairs(targets, partners, weights, at_weights, side, sums=(), before=()):
    count, late = len(partners), len(targets) == 1
    half = side // 2
    tiles = side * side // LANES
    pairs = count * len(targets)
    rows = pairs * side**3 // LANES
    back = rows if late else rows // 2
    lane = lane_table(side)
    tables = [
        jnp.asarray(bf16_parts(lane)),
        jnp.asarray(bf16_parts(lane.T)),
        jnp.asarray(twist_table(side, SUBLANES)),
        jnp.asarray(turn_table(side)),
    ]
    operands = [x for pair in partners for x in pair] + [x for pair in targets for x in pair]
    operands += [weights, *tables, *sums, *before]
    size = 2 * tiles * half + 8
    sizes = [size, tiles * half + 8, tiles * half] if late else [size, size, 8]
    messages = tuple(jax.ShapeDtypeStruct((n, LANES), F32) for n in sizes)
    return pl.pallas_call(
        functools.partial(pair_kernel, side, count, at_weights, late, len(sums) > 0),
        out_shape=messages,
        in_specs=[VMEM] * len(operands),
        out_specs=(VMEM,) * len(messages),
        scratch_shapes=[
            pltpu.VMEM((rows // SUBLANES * STEP, LANES), F32),
            pltpu.VMEM((rows // SUBLANES * STEP, LANES), F32),
            pltpu.VMEM((rows, 2 * LANES), BF16),
            pltpu.VMEM((rows, 2 * LANES), BF16),
            pltpu.VMEM((rows, 2 * LANES), F32),
            pltpu.VMEM((back, 2 * LANES), BF16),
            pltpu.VMEM((back, 2 * LANES), BF16),
            pltpu.VMEM((back, 2 * LANES), F32),
        ],
        compiler_params=params(),
        cost_estimate=LATE_COST if late else COST,
        name="pairs",
    )(*operands)


def join(parts, shape):
    applied, gram = pl.pallas_call(
        join_kernel,
        out_shape=(jax.ShapeDtypeStruct(shape, F32), jax.ShapeDtypeStruct((1, 1, 2), F32)),
        in_specs=[VMEM] * len(parts),
        out_specs=(VMEM, SMEM),
        compiler_params=params(),
        cost_estimate=COST,
        name="join",
    )(*parts)
    return applied, gram.transpose(2, 0, 1)


def block_gram(orbitals, applied, owner, blocks_per_k, cells):
    highest = lax.Precision.HIGHEST
    partners = lax.all_gather(orbitals, "kb", axis=1, tiled=True)
    re = jnp.einsum("pxa,txa->tp", partners[0], applied[0], precision=highest)
    re += jnp.einsum("pxa,txa->tp", partners[1], applied[1], precision=highest)
    im = jnp.einsum("pxa,txa->tp", partners[0], applied[1], precision=highest)
    im -= jnp.einsum("pxa,txa->tp", partners[1], applied[0], precision=highest)
    sums = lax.psum(jnp.stack([re, im]) / cells, "slab")
    own = owner[lax.axis_index("kb")] // blocks_per_k
    wanted = own * blocks_per_k + jnp.arange(blocks_per_k, dtype=jnp.int32)
    selector = jnp.where(owner[:, None] == wanted[None], 1.0, 0.0).astype(F32)
    return jnp.einsum("ktp,pc->ktc", sums, selector, precision=highest)


def on_device(orbitals, kernel, q_index, owner):
    side = kernel.shape[1]
    n_kb = lax.axis_size("kb")
    lines = n_kb // 2
    blocks_per_k = n_kb // NK
    across = [(a, a ^ 1) for a in range(n_kb)]

    def swap(x):
        return lax.ppermute(x, "slab", [(0, 1), (1, 0)])

    def from_line(x, d):
        return lax.ppermute(
            x, "kb", [(2 * a + c, 2 * (a ^ d) + c) for a in range(lines) for c in range(2)]
        )

    late = 3 if lines == 4 else None
    order = [d for d in range(lines) if d != late]
    first = [*order[2:], 1, 0]
    own = (orbitals, swap(orbitals))
    arrived = {d: from_line(orbitals, d) for d in order[1:]}
    arrived[0] = lax.ppermute(orbitals, "kb", across)
    weights = choose_weights(
        q_index, owner, (kernel, swap(kernel)), tuple(order), late, side, blocks_per_k
    )
    landed = lax.optimization_barrier((*(arrived[d] for d in first), weights))
    arrived.update(zip(first, landed))
    weights = landed[-1]
    far = {d: swap(arrived[d]) for d in first}
    beside = (arrived[0], far[0])
    partners = [own] + [(arrived[d], far[d]) for d in order[1:]]
    sums = ()
    for at in range(0, len(order), 4):
        at_weights = (at, len(order) + at)
        sums = apply_pairs(
            (own, beside), partners[at : at + 4], weights, at_weights, side, sums[:2]
        )
    if late is not None:
        steps = (2 * late, 2 * late + 1)
        moves = [(2 * a + c, 2 * (a ^ steps[c]) + c) for a in range(n_kb) for c in range(2)]
        last = lax.ppermute(jnp.concatenate(own), ("kb", "slab"), moves)
        last, _ = lax.optimization_barrier((last, sums))
    home, away, away_sums = sums
    parts = [home, lax.ppermute(away, "kb", across)]
    if late is not None:
        crossed = [(2 * a + c, 2 * (a ^ 1) + 1 - c) for a in range(n_kb) for c in range(2)]
        crossed_sums = lax.ppermute(away_sums, ("kb", "slab"), crossed)
        late_mine, *late_rows = apply_pairs(
            (own,), [(last,)], weights, (2 * len(order),), side, before=(home, crossed_sums)
        )
        parts += [late_mine, *(swap(x) for x in late_rows)]
    applied, gram = join(parts, orbitals.shape)
    if blocks_per_k > 1:
        gram = block_gram(orbitals, applied, owner, blocks_per_k, side**3)
    return applied, gram


def solution(mesh):
    in_specs = (P(None, ("grp", "kb"), "slab", None), P(None, None, "slab"), P(), P())
    out_specs = (P(None, ("grp", "kb"), "slab", None), P(None, ("grp", "kb"), None))
    return jax.shard_map(
        on_device, mesh=mesh, in_specs=in_specs, out_specs=out_specs, check_vma=False
    )
```

```python
import functools
import math

import jax
import jax.numpy as jnp
import numpy as np
from jax import lax
from jax.experimental import pallas as pl
from jax.experimental.pallas import tpu as pltpu
from jax.sharding import PartitionSpec as P

NK = 8
SUBLANES = 8
MARGIN = 24
STEP = 9
GROUP = 4
LANES = 128
F32 = jnp.float32
BF16 = jnp.bfloat16


def bf16_parts(table):
    high = table.astype(np.float32).astype(BF16)
    low = (table - high.astype(np.float64)).astype(np.float32).astype(BF16)
    return np.stack([high, low])


def lane_table(side):
    lows = LANES // side
    index = np.arange(LANES)
    low, z = index // side, index % side
    phase = 2.0 * math.pi * (np.outer(low, low) / lows + np.outer(z, z) / side)
    real, imag = np.cos(phase), -np.sin(phase)
    return np.block([[real, imag], [-imag, real]])


def turn_table(side):
    phase = 2.0 * math.pi * np.arange(side // 2) / side
    both = np.stack([np.cos(phase), np.sin(phase)]).astype(np.float32)
    return np.ascontiguousarray(np.broadcast_to(both[..., None], (*both.shape, LANES)))


def twist_table(side, rows):
    tiles = side * side // LANES
    phase = 2.0 * math.pi * np.outer(np.arange(tiles), np.arange(LANES) // side) / side
    both = np.stack([np.cos(phase), np.sin(phase)], 1).astype(np.float32)
    return np.ascontiguousarray(np.broadcast_to(both[:, :, None], (tiles, 2, rows, LANES)))


def split(value):
    high = value.astype(BF16)
    return high, (value - high.astype(F32)).astype(BF16)


def dot_parts(left, right):
    dot = functools.partial(jnp.dot, preferred_element_type=F32)
    return dot(left[0], right[0]) + (dot(left[1], right[0]) + dot(left[0], right[1]))


def dft_list(values, sign):
    count = len(values)
    if count == 1:
        return values
    even, odd = dft_list(values[0::2], sign), dft_list(values[1::2], sign)
    first, second = [], []
    for k in range(count // 2):
        re, im = odd[k]
        eighth = 8 * k // count if 8 * k % count == 0 else None
        if eighth == 0:
            pass
        elif eighth == 2:
            re, im = (-im, re) if sign > 0 else (im, -re)
        elif eighth == 1:
            root = math.sqrt(0.5)
            re, im = (
                ((re - im) * root, (re + im) * root)
                if sign > 0
                else ((re + im) * root, (im - re) * root)
            )
        elif eighth == 3:
            root = math.sqrt(0.5)
            re, im = (
                ((-re - im) * root, (re - im) * root)
                if sign > 0
                else ((im - re) * root, (-re - im) * root)
            )
        else:
            angle = 2.0 * math.pi * k / count
            cosine, sine = math.cos(angle), sign * math.sin(angle)
            re, im = re * cosine - im * sine, re * sine + im * cosine
        first.append((even[k][0] + re, even[k][1] + im))
        second.append((even[k][0] - re, even[k][1] - im))
    return first + second


def lane_slice(tile):
    return pl.ds(tile * LANES, LANES)


def weight_kernel(side, blocks_per_k, order, late, q_ref, owner_ref, mine_ref, other_ref, weight_ref):
    tiles = side * side // LANES
    lows = LANES // side
    scale = -1.0 / (NK * side**3)
    place, core = lax.axis_index("kb"), lax.axis_index("slab")
    line, column = place // 2, place % 2
    first_core = core == 0
    lane = lax.broadcasted_iota(jnp.int32, (side, LANES), 1) // side
    targets = (place, place ^ 1)
    pairs = [(target, 2 * (line ^ d) + column) for target in targets for d in order]
    if late is not None:
        pairs.append((place, 2 * (line ^ late) + (column ^ core)))
    for pair, (target_at, partner_at) in enumerate(pairs):
        q = q_ref[owner_ref[target_at] // blocks_per_k, owner_ref[partner_at] // blocks_per_k]
        mine, other = mine_ref[q], other_ref[q]
        low_half = jnp.where(first_core, mine, other) * scale
        high_half = jnp.where(first_core, other, mine) * scale
        for b in range(tiles):
            total = None
            for a in range(lows):
                row = a * tiles + b
                source, chunk = row // lows, row % lows
                half = low_half if source < tiles // 2 else high_half
                at = source % (tiles // 2) * LANES
                piece = half[:, at : at + LANES]
                shift = (a - chunk) % lows * side
                if shift:
                    piece = pltpu.roll(piece, shift, 1)
                total = piece if total is None else jnp.where(lane == a, piece, total)
            at = pl.ds(b // GROUP * GROUP * side + b % GROUP, side, stride=GROUP)
            weight_ref[pair, at, :] = total


def pair_kernel(side, count, at_weights, late, has_sum, *refs):
    refs = list(refs)
    take = lambda n: [refs.pop(0) for _ in range(n)]
    partners = [take(1 if late else 2) for _ in range(count)]
    targets = [take(2) for _ in range(1 if late else 2)]
    (weight_ref,) = take(1)
    lane_f, lane_b, twist, turn = take(4)
    sums = take(2) if has_sum else None
    before = take(2) if late else None
    outs = take(2 if late else 3)
    x_re, x_im, high_ref, low_ref, f_ref, back_high, back_low, g_ref = take(8)
    if late:
        partners = [[whole.at[0:2], whole.at[2:4]] for (whole,) in partners]

    tiles = side * side // LANES
    half = side // 2
    subs = 2 * GROUP
    rows = half * subs
    groups = tiles // GROUP
    halves = 2 if late else 1

    def parts(ref):
        return ref[0], ref[1]

    def field(band, h, block, t):
        return band[h][0, 0, block, lane_slice(t)], band[h][1, 0, block, lane_slice(t)]

    def spread(pair, b, x, parity):
        start = ((pair * groups + b // GROUP) * half + x) * STEP + parity * GROUP + b % GROUP
        return pl.ds(start, SUBLANES, stride=STEP)

    def packed(g, x):
        return pl.ds((g * half + x) * STEP, subs)

    def densities(pair, target, partner):
        for x in range(0, half, SUBLANES):
            block = pl.ds(x, SUBLANES)
            both = []
            for h in range(2):
                values = []
                for t in range(tiles):
                    t_re, t_im = field(target, h, block, t)
                    p_re, p_im = field(partner, h, block, t)
                    values.append((p_re * t_re + p_im * t_im, p_re * t_im - p_im * t_re))
                both.append(dft_list(values, -1))
            turn_re, turn_im = turn[0, block], turn[1, block]
            for b in range(tiles):
                (re_0, im_0), (re_1, im_1) = both[0][b], both[1][b]
                re, im = re_0 - re_1, im_0 - im_1
                even = re_0 + re_1, im_0 + im_1
                odd = re * turn_re + im * turn_im, im * turn_re - re * turn_im
                for parity, (re, im) in enumerate((even, odd)):
                    if b:
                        cosine, sine = twist[b, 0], twist[b, 1]
                        re, im = re * cosine + im * sine, im * cosine - re * sine
                    x_re[spread(pair, b, x, parity), :] = re
                    x_im[spread(pair, b, x, parity), :] = im

    def transform(g, weights):
        values = [(x_re[packed(g, x), :], x_im[packed(g, x), :]) for x in range(half)]
        values = dft_list(values, -1)
        for x in range(0, half, 2):
            at = pl.ds(g * rows + x * subs, 2 * subs)
            for k in range(2):
                high, low = split(jnp.concatenate([values[x][k], values[x + 1][k]], 0))
                high_ref[at, lane_slice(k)] = high
                low_ref[at, lane_slice(k)] = low
        at = pl.ds(g * rows, rows)
        spectrum = dot_parts((high_ref[at, :], low_ref[at, :]), parts(lane_f))
        f_ref[at, :] = spectrum * jnp.concatenate([weights, weights], 1)
        values = []
        for x in range(half):
            at = pl.ds(g * rows + x * subs, subs)
            values.append((f_ref[at, lane_slice(0)], f_ref[at, lane_slice(1)]))
        for x, (re, im) in enumerate(dft_list(values, 1)):
            x_re[packed(g, x), :] = re
            x_im[packed(g, x), :] = im

    def potentials(pair):
        for b in range(tiles):
            made = [[] for _ in range(halves)]
            for x in range(0, half, SUBLANES):
                block = pl.ds(x, SUBLANES)
                turn_re, turn_im = turn[0, block], turn[1, block]
                even_re, even_im = x_re[spread(pair, b, x, 0), :], x_im[spread(pair, b, x, 0), :]
                re, im = x_re[spread(pair, b, x, 1), :], x_im[spread(pair, b, x, 1), :]
                re, im = re * turn_re - im * turn_im, im * turn_re + re * turn_im
                made[0].append((even_re + re, even_im + im))
                if late:
                    made[1].append((even_re - re, even_im - im))
            for h in range(halves):
                at = pl.ds(((pair * halves + h) * tiles + b) * half, half)
                for k in range(2):
                    high, low = split(jnp.concatenate([block[k] for block in made[h]], 0))
                    back_high[at, lane_slice(k)] = high
                    back_low[at, lane_slice(k)] = low
        at = pl.ds(pair * halves * tiles * half, halves * tiles * half)
        g_ref[at, :] = dot_parts((back_high[at, :], back_low[at, :]), parts(lane_b))

    pairs = [(c, p) for c in range(len(targets)) for p in range(count)]
    for pair, (c, p) in enumerate(pairs):
        densities(pair, targets[c], partners[p])
    for pair, (c, p) in enumerate(pairs):
        for g in range(groups):
            weights = weight_ref[at_weights[c] + p, pl.ds(g * rows, rows), :]
            transform(pair * groups + g, weights)
    for pair in range(len(pairs)):
        potentials(pair)
    for c, target in enumerate(targets):
        gram_re = jnp.zeros((SUBLANES, LANES), F32)
        gram_im = jnp.zeros((SUBLANES, LANES), F32)
        for h in range(halves):
            for x in range(0, half, SUBLANES):
                block = pl.ds(x, SUBLANES)
                total = [[0.0, 0.0] for _ in range(tiles)]
                if has_sum:
                    for t in range(tiles):
                        for k in range(2):
                            total[t][k] = sums[c][pl.ds((k * tiles + t) * half + x, SUBLANES), :]
                for p, partner in enumerate(partners):
                    values = []
                    for b in range(tiles):
                        pair = c * count + p
                        start = ((pair * halves + h) * tiles + b) * half + x
                        at = pl.ds(start, SUBLANES)
                        re, im = g_ref[at, lane_slice(0)], g_ref[at, lane_slice(1)]
                        if b:
                            cosine, sine = twist[b, 0], twist[b, 1]
                            re, im = re * cosine - im * sine, im * cosine + re * sine
                        values.append((re, im))
                    for t, (re, im) in enumerate(dft_list(values, 1)):
                        p_re, p_im = field(partner, h, block, t)
                        total[t][0] = total[t][0] + (p_re * re - p_im * im)
                        total[t][1] = total[t][1] + (p_re * im + p_im * re)
                for t in range(tiles):
                    re, im = total[t]
                    t_re, t_im = field(target, h, block, t)
                    gram_re += t_re * re + t_im * im
                    gram_im += t_re * im - t_im * re
                    outs[h + c][pl.ds(t * half + x, SUBLANES), :] = re
                    outs[h + c][pl.ds((tiles + t) * half + x, SUBLANES), :] = im
        end = 2 * tiles * half
        scale = 1.0 / side**3
        sums_row = jnp.concatenate(
            [
                jnp.full((4, LANES), jnp.sum(gram_re) * scale, F32),
                jnp.full((4, LANES), jnp.sum(gram_im) * scale, F32),
            ],
            0,
        )
        if late:
            sums_row += before[0][pl.ds(end, 8), :] + before[1][...]
            outs[0][pl.ds(end, 8), :] = sums_row
            outs[1][pl.ds(end, 8), :] = sums_row
        else:
            outs[c][pl.ds(end, 8), :] = sums_row
            if c:
                outs[1][pl.ds(end + 8, MARGIN), :] = jnp.zeros((MARGIN, LANES), F32)
                outs[2][...] = sums_row


def join_kernel(*refs):
    home, away, *late, applied_ref, gram_ref = refs
    half = applied_ref.shape[2]
    tiles = applied_ref.shape[3] // LANES
    for k in range(2):
        for t in range(tiles):
            at = pl.ds((k * tiles + t) * half, half)
            found = home[at, :] + away[at, :]
            if late:
                found += late[0][at, :] + late[1][at, :]
            applied_ref[k, 0, :, lane_slice(t)] = found
    if late:
        gram = late[0][pl.ds(2 * tiles * half, 8), :] + late[1][pl.ds(2 * tiles * half, 8), :]
    else:
        gram = home[pl.ds(2 * tiles * half, 8), :]
    gram_ref[0, 0, 0] = jnp.max(gram[0:1, :])
    gram_ref[0, 0, 1] = jnp.max(gram[4:5, :])


VMEM = pl.BlockSpec(memory_space=pltpu.VMEM)
SMEM = pl.BlockSpec(memory_space=pltpu.SMEM)


COST = pl.CostEstimate(flops=1, bytes_accessed=1, transcendentals=0)

LATE_COST = pl.CostEstimate(flops=2 * 10**9, bytes_accessed=4 * 2**20, transcendentals=0)


def params():
    return pltpu.CompilerParams(vmem_limit_bytes=48 * 2**20)


def choose_weights(q_index, owner, kernels, order, late, side, blocks_per_k):
    count = 2 * len(order) + (late is not None)
    return pl.pallas_call(
        functools.partial(weight_kernel, side, blocks_per_k, order, late),
        out_shape=jax.ShapeDtypeStruct((count, side**3 // LANES, LANES), F32),
        in_specs=[SMEM, SMEM, VMEM, VMEM],
        out_specs=VMEM,
        compiler_params=params(),
        cost_estimate=COST,
        name="weights",
    )(q_index, owner, *kernels)


def apply_pairs(targets, partners, weights, at_weights, side, sums=(), before=()):
    count, late = len(partners), len(targets) == 1
    half = side // 2
    tiles = side * side // LANES
    pairs = count * len(targets)
    rows = pairs * side**3 // LANES
    back = rows if late else rows // 2
    lane = lane_table(side)
    tables = [
        jnp.asarray(bf16_parts(lane)),
        jnp.asarray(bf16_parts(lane.T)),
        jnp.asarray(twist_table(side, SUBLANES)),
        jnp.asarray(turn_table(side)),
    ]
    operands = [x for pair in partners for x in pair] + [x for pair in targets for x in pair]
    operands += [weights, *tables, *sums, *before]
    size = 2 * tiles * half + 8
    sizes = [size, size] if late else [size, size + MARGIN, 8]
    messages = tuple(jax.ShapeDtypeStruct((n, LANES), F32) for n in sizes)
    return pl.pallas_call(
        functools.partial(pair_kernel, side, count, at_weights, late, len(sums) > 0),
        out_shape=messages,
        in_specs=[VMEM] * len(operands),
        out_specs=(VMEM,) * len(messages),
        scratch_shapes=[
            pltpu.VMEM((rows // SUBLANES * STEP, LANES), F32),
            pltpu.VMEM((rows // SUBLANES * STEP, LANES), F32),
            pltpu.VMEM((rows, 2 * LANES), BF16),
            pltpu.VMEM((rows, 2 * LANES), BF16),
            pltpu.VMEM((rows, 2 * LANES), F32),
            pltpu.VMEM((back, 2 * LANES), BF16),
            pltpu.VMEM((back, 2 * LANES), BF16),
            pltpu.VMEM((back, 2 * LANES), F32),
        ],
        compiler_params=params(),
        cost_estimate=LATE_COST if late else COST,
        name="pairs",
    )(*operands)


def join(parts, shape):
    applied, gram = pl.pallas_call(
        join_kernel,
        out_shape=(jax.ShapeDtypeStruct(shape, F32), jax.ShapeDtypeStruct((1, 1, 2), F32)),
        in_specs=[VMEM] * len(parts),
        out_specs=(VMEM, SMEM),
        compiler_params=params(),
        cost_estimate=COST,
        name="join",
    )(*parts)
    return applied, gram.transpose(2, 0, 1)


def block_gram(orbitals, applied, owner, blocks_per_k, cells):
    highest = lax.Precision.HIGHEST
    partners = lax.all_gather(orbitals, "kb", axis=1, tiled=True)
    re = jnp.einsum("pxa,txa->tp", partners[0], applied[0], precision=highest)
    re += jnp.einsum("pxa,txa->tp", partners[1], applied[1], precision=highest)
    im = jnp.einsum("pxa,txa->tp", partners[0], applied[1], precision=highest)
    im -= jnp.einsum("pxa,txa->tp", partners[1], applied[0], precision=highest)
    sums = lax.psum(jnp.stack([re, im]) / cells, "slab")
    own = owner[lax.axis_index("kb")] // blocks_per_k
    wanted = own * blocks_per_k + jnp.arange(blocks_per_k, dtype=jnp.int32)
    selector = jnp.where(owner[:, None] == wanted[None], 1.0, 0.0).astype(F32)
    return jnp.einsum("ktp,pc->ktc", sums, selector, precision=highest)


def on_device(orbitals, kernel, q_index, owner):
    side = kernel.shape[1]
    n_kb = lax.axis_size("kb")
    lines = n_kb // 2
    blocks_per_k = n_kb // NK
    across = [(a, a ^ 1) for a in range(n_kb)]

    def swap(x):
        return lax.ppermute(x, "slab", [(0, 1), (1, 0)])

    def from_line(x, d):
        return lax.ppermute(
            x, "kb", [(2 * a + c, 2 * (a ^ d) + c) for a in range(lines) for c in range(2)]
        )

    late = 3 if lines == 4 else None
    order = [d for d in range(lines) if d != late]
    first = [*order[2:], 1, 0]
    own = (orbitals, swap(orbitals))
    arrived = {d: from_line(orbitals, d) for d in order[1:]}
    arrived[0] = lax.ppermute(orbitals, "kb", across)
    weights = choose_weights(
        q_index, owner, (kernel, swap(kernel)), tuple(order), late, side, blocks_per_k
    )
    landed = lax.optimization_barrier((*(arrived[d] for d in first), weights))
    arrived.update(zip(first, landed))
    weights = landed[-1]
    far = {d: swap(arrived[d]) for d in first}
    beside = (arrived[0], far[0])
    partners = [own] + [(arrived[d], far[d]) for d in order[1:]]
    sums = ()
    for at in range(0, len(order), 4):
        at_weights = (at, len(order) + at)
        sums = apply_pairs(
            (own, beside), partners[at : at + 4], weights, at_weights, side, sums[:2]
        )
    if late is not None:
        steps = (2 * late, 2 * late + 1)
        moves = [(2 * a + c, 2 * (a ^ steps[c]) + c) for a in range(n_kb) for c in range(2)]
        last = lax.ppermute(jnp.concatenate(own), ("kb", "slab"), moves)
        last, _ = lax.optimization_barrier((last, sums))
    home, away, away_sums = sums
    parts = [home, lax.ppermute(away, "kb", across)]
    if late is not None:
        crossed = [(2 * a + c, 2 * (a ^ 1) + 1 - c) for a in range(n_kb) for c in range(2)]
        crossed_sums = lax.ppermute(away_sums, ("kb", "slab"), crossed)
        late_mine, *late_rows = apply_pairs(
            (own,), [(last,)], weights, (2 * len(order),), side, before=(home, crossed_sums)
        )
        parts += [late_mine, *(swap(x) for x in late_rows)]
    applied, gram = join(parts, orbitals.shape)
    if blocks_per_k > 1:
        gram = block_gram(orbitals, applied, owner, blocks_per_k, side**3)
    return applied, gram


def solution(mesh):
    in_specs = (P(None, ("grp", "kb"), "slab", None), P(None, None, "slab"), P(), P())
    out_specs = (P(None, ("grp", "kb"), "slab", None), P(None, ("grp", "kb"), None))
    return jax.shard_map(
        on_device, mesh=mesh, in_specs=in_specs, out_specs=out_specs, check_vma=False
    )
```
